32 devices in a mesh: context: 8 (over y, x, core), chan: 4 (over z).
Axes of the slice: x: 2, y: 2, z: 4, core: 2. Of those that a mesh axis runs over, the one named last changes fastest.
Arguments:
- signal: float32 [64, 8192], P('chan', 'context'), may hold values from -6 to 6
- filter_taps: float32 [8192], P('context'), may hold values from -6 to 6
- skip_gain: float32 [64], P('chan'), may hold values from 0.5 to 1.5
- cotangent: float32 [64, 8192], P('chan', 'context'), may hold values from -6 to 6
Outputs:
- output: float32 [64, 8192], P('chan', 'context')
- grad_signal: float32 [64, 8192], P('chan', 'context')
- grad_filter: float32 [8192], P('context')
The draws below stay inside these ranges and needn't reach their ends.
All inputs are finite; a program needn't handle non-finite values.
Results may differ from the reference program's by a relative error of at most 0.00013.
Values sent between devices are 32-bit elements; how exact they have to be, the bound alone decides.
No kernel may reach another device: no remote copies, remote signals or barrier semaphores. Data moves between devices by JAX's collectives and lax.ppermute only.
A program may use at most 64 MiB of HBM per device.

```python
import math
import jax
import jax.numpy as jnp
from jax import lax

CH = 64
SEQ = 8192


def level_of(rng, extent, cuts, smallest, top_value):
    level, own = 1.0, jax.random.fold_in(rng, 6)
    for axis_at, shards_of in cuts:
        steps = jnp.exp(jax.random.uniform(jax.random.fold_in(own, axis_at), (shards_of,), jnp.float32, smallest / len(cuts), top_value / len(cuts)))
        level = level * jnp.repeat(steps, extent[axis_at] // shards_of).reshape([-1 if axis == axis_at else 1 for axis in range(len(extent))])
    return level


def scatter_about(stream_key, dims, deviation, bound, split=(), kind=jnp.bfloat16):
    loudness = level_of(stream_key, dims, split, -0.22, 0.18) if split else 1.0
    values = jax.random.normal(stream_key, dims, jnp.float32) * deviation * loudness
    return jnp.minimum(jnp.maximum(values, -bound), bound).astype(kind)


def setup_inputs(seed: int = 0) -> dict:
    key_list = jax.random.split(jax.random.key(seed), 5)
    return {
        "signal": scatter_about(key_list[0], (CH, SEQ), 1.0, 6.0, ((0, 4), (1, 8)), jnp.float32),
        "filter_taps": scatter_about(key_list[1], (SEQ,), 1.0, 6.0, ((0, 8),), jnp.float32),
        "skip_gain": jnp.clip(0.5 + 1.0 * jax.random.uniform(key_list[2], (CH,), jnp.float32) ** level_of(key_list[2], (CH,), ((0, 4),), -0.2, 0.2), 0.5, 1.5),
        "cotangent": scatter_about(key_list[3], (CH, SEQ), 1.0, 6.0, ((0, 4), (1, 8)), jnp.float32),
    }


def reference(signal, filter_taps, skip_gain, cotangent):
    period = 2 * SEQ
    factor = 1.0 / math.sqrt(SEQ)
    spec_signal = jnp.fft.rfft(signal, n=period, axis=-1)
    spec_filter = jnp.fft.rfft(filter_taps, n=period)
    spec_cot = jnp.fft.rfft(cotangent, n=period, axis=-1)
    conv = jnp.fft.irfft(spec_signal * spec_filter[None, :], n=period, axis=-1)[:, :SEQ]
    output = (conv * factor + skip_gain[:, None] * signal).astype(jnp.float32)
    back = jnp.fft.irfft(spec_cot * jnp.conj(spec_filter)[None, :], n=period, axis=-1)[:, :SEQ]
    grad_signal = (back * factor + skip_gain[:, None] * cotangent).astype(jnp.float32)
    summed = lax.optimization_barrier(jnp.sum(spec_cot * jnp.conj(spec_signal), axis=0))
    grad_filter = (jnp.fft.irfft(summed, n=period)[:SEQ] * factor).astype(jnp.float32)
    return (output, grad_signal, grad_filter)
```

```python
import functools
import math

import jax
import jax.numpy as jnp
from jax import lax
from jax.experimental import pallas as pl
from jax.experimental.pallas import tpu as pltpu
from jax.sharding import PartitionSpec as P

exact_mode = lax.Precision.HIGHEST

LANES = 128
BLOCK = 256
PACKED_ROWS = 16
KERNEL_BYTES = 48 * 1024 * 1024


def halves(value):
    high = value.astype(jnp.bfloat16)
    low = (value - high.astype(jnp.float32)).astype(jnp.bfloat16)
    return high, low


def dot(left, right, left_dim, right_dim):
    return lax.dot_general(
        left, right, (((left_dim,), (right_dim,)), ((), ())), preferred_element_type=jnp.float32
    )


def dot_halves(left, right, left_dim, right_dim):
    return (
        dot(left[0], right[0], left_dim, right_dim)
        + dot(left[0], right[1], left_dim, right_dim)
        + dot(left[1], right[0], left_dim, right_dim)
    )


def stack_kernel(signal_ref, cotangent_ref, taps_ref, out_ref):
    channels, tokens = signal_ref.shape
    row = 0
    for source in (signal_ref, cotangent_ref):
        for tile in range(tokens // LANES):
            out_ref[row : row + channels, :] = source[:, tile * LANES : (tile + 1) * LANES]
            row += channels
    out_ref[row:, :] = taps_ref[...]


def stack_local(signal, cotangent, taps):
    channels, tokens = signal.shape
    rows = (2 * channels * tokens + tokens) // LANES
    return pl.pallas_call(
        stack_kernel,
        out_shape=jax.ShapeDtypeStruct((rows, LANES), jnp.float32),
        in_specs=[pl.BlockSpec(memory_space=pltpu.VMEM)] * 3,
        out_specs=pl.BlockSpec(memory_space=pltpu.VMEM),
        name="stack_local",
    )(signal, cotangent, taps.reshape(tokens // LANES, LANES))


def gather_blocks(stacked, shards):
    def flipped(value, bits):
        return lax.ppermute(value, "context", [(i, i ^ bits) for i in range(shards)])

    found = {0: stacked}
    for bits in range(2, shards, 2):
        found[bits] = flipped(stacked, bits)
    for bits in range(0, shards, 2):
        found[bits + 1] = flipped(found[bits], 1)
    return [found[bits] for bits in range(shards)]


def place_rows(block_ref, index, channels, tokens, first, high_ref, low_ref, start):
    per = tokens // BLOCK
    for tile in range(tokens // LANES):
        rows = first + tile * channels
        high, low = halves(block_ref[rows : rows + channels, :])
        at = pl.multiple_of((index * per + tile // 2) * channels + start, PACKED_ROWS)
        lanes = slice((tile % 2) * LANES, (tile % 2 + 1) * LANES)
        high_ref[pl.ds(at, channels), lanes] = high
        low_ref[pl.ds(at, channels), lanes] = low


def filter_grad_kernel(shards, channels, tokens, *refs):
    blocks, out_ref = refs[:shards], refs[shards]
    sig_high, sig_low, cot_high, cot_low, folded = refs[shards + 1 :]
    me = lax.axis_index("context")
    per = tokens // BLOCK
    rows = shards * per * channels
    cot_high[rows:, :] = jnp.zeros((rows, BLOCK), jnp.bfloat16)
    cot_low[rows:, :] = jnp.zeros((rows, BLOCK), jnp.bfloat16)
    for bits in range(shards):
        index = me ^ bits
        place_rows(blocks[bits], index, channels, tokens, 0, sig_high, sig_low, 0)
        place_rows(
            blocks[bits], index, channels, tokens, channels * tokens // LANES, cot_high, cot_low, 0
        )
    sig = (sig_high[...], sig_low[...])
    for lag in range(per + 1):
        at = pl.multiple_of((me * per + lag) * channels, PACKED_ROWS)
        window = (cot_high[pl.ds(at, rows), :], cot_low[pl.ds(at, rows), :])
        folded[:, lag * BLOCK : (lag + 1) * BLOCK] = dot_halves(sig, window, 0, 0)
    width = (per + 1) * BLOCK - LANES
    total = None
    for group in range(LANES // 8):
        part = (
            folded[8 * group : 8 * group + 8, :width]
            + folded[LANES + 8 * group : LANES + 8 * group + 8, LANES:]
        )
        if group:
            part = pltpu.roll(part, width - 8 * group, 1)
        total = part if total is None else total + part
    row = lax.broadcasted_iota(jnp.int32, total.shape, 0)
    for step in (1, 2, 4):
        total = jnp.where((row & step) != 0, pltpu.roll(total, width - step, 1), total)
    out_ref[...] = jnp.sum(total, axis=0, keepdims=True)[:, :tokens]


def filter_grad(blocks, shards, channels, tokens):
    rows = shards * tokens // BLOCK * channels
    per = tokens // BLOCK
    return pl.pallas_call(
        functools.partial(filter_grad_kernel, shards, channels, tokens),
        out_shape=jax.ShapeDtypeStruct((1, tokens), jnp.float32),
        in_specs=[pl.BlockSpec(memory_space=pltpu.VMEM)] * shards,
        out_specs=pl.BlockSpec(memory_space=pltpu.VMEM),
        scratch_shapes=[
            pltpu.VMEM((rows, BLOCK), jnp.bfloat16),
            pltpu.VMEM((rows, BLOCK), jnp.bfloat16),
            pltpu.VMEM((2 * rows, BLOCK), jnp.bfloat16),
            pltpu.VMEM((2 * rows, BLOCK), jnp.bfloat16),
            pltpu.VMEM((BLOCK, (per + 1) * BLOCK), jnp.float32),
        ],
        compiler_params=pltpu.CompilerParams(vmem_limit_bytes=KERNEL_BYTES),
        cost_estimate=pl.CostEstimate(
            flops=2 * 3 * (per + 1) * rows * BLOCK * BLOCK, bytes_accessed=4 * rows * BLOCK * 2, transcendentals=0
        ),
        name="filter_grad",
    )(*blocks)


def convolve_kernel(shards, channels, tokens, *refs):
    blocks, gain_ref, out_ref, back_ref = refs[:shards], *refs[shards : shards + 3]
    sig_high, sig_low, cot_high, cot_low, taps, toe_high, toe_low = refs[shards + 3 :]
    me = lax.axis_index("context")
    per = tokens // BLOCK
    rows = shards * per * channels
    tiles = tokens // LANES
    for ref in (sig_high, sig_low):
        ref[:rows, :] = jnp.zeros((rows, BLOCK), jnp.bfloat16)
    for ref in (cot_high, cot_low):
        ref[rows:, :] = jnp.zeros((rows, BLOCK), jnp.bfloat16)
    for bits in range(shards):
        index = me ^ bits
        place_rows(blocks[bits], index, channels, tokens, 0, sig_high, sig_low, rows)
        place_rows(
            blocks[bits], index, channels, tokens, channels * tiles, cot_high, cot_low, 0
        )
        taps[pl.ds(pl.multiple_of(index * tiles, 8), tiles), :] = blocks[bits][2 * channels * tiles :, :]
    row = lax.broadcasted_iota(jnp.int32, (8, LANES), 0)
    lane = lax.broadcasted_iota(jnp.int32, (8, LANES), 1)
    groups = LANES // 8
    toe_high[0] = jnp.zeros((LANES, LANES), jnp.bfloat16)
    toe_low[0] = jnp.zeros((LANES, LANES), jnp.bfloat16)

    def build(step, carry):
        last, rolled = carry
        sheet = taps[pl.ds(pl.multiple_of(step * 8, 8), 8), :]
        for line in range(8):
            now = jnp.broadcast_to(sheet[line : line + 1, :], (8, LANES))
            for bit in (1, 2, 4):
                now = jnp.where((row & bit) != 0, pltpu.roll(now, bit, 1), now)
            skewed = jnp.where(lane < row, last, now)
            last = now
            turned = [skewed] + [pltpu.roll(skewed, 8 * g, 1) for g in range(1, groups)]
            parts = [turned[0]] + [
                jnp.where(lane < 8 * g, rolled[g], turned[g]) for g in range(1, groups)
            ]
            rolled = turned
            high, low = halves(jnp.concatenate(parts, axis=0))
            toe_high[step * 8 + line + 1] = high
            toe_low[step * 8 + line + 1] = low
        return last, rolled

    blank = jnp.zeros((8, LANES), jnp.float32)
    lax.fori_loop(0, shards * tiles // 8, build, (blank, [blank] * groups))

    def square(ref, step):
        return jnp.concatenate(
            [
                jnp.concatenate([ref[2 * step + 1], ref[2 * step + 2]], axis=1),
                jnp.concatenate([ref[2 * step], ref[2 * step + 1]], axis=1),
            ],
            axis=0,
        )

    def forward(trip, total):
        for inner in range(per):
            step = trip * per + inner
            at = pl.multiple_of(rows + (me * per - step) * channels, PACKED_ROWS)
            window = (sig_high[pl.ds(at, per * channels), :], sig_low[pl.ds(at, per * channels), :])
            total = total + dot_halves(window, (square(toe_high, step), square(toe_low, step)), 1, 0)
        return total

    def backward(trip, total):
        for inner in range(per):
            step = trip * per + inner
            at = pl.multiple_of((me * per + step) * channels, PACKED_ROWS)
            window = (cot_high[pl.ds(at, per * channels), :], cot_low[pl.ds(at, per * channels), :])
            total = total + dot_halves(window, (square(toe_high, step), square(toe_low, step)), 1, 1)
        return total

    start = jnp.zeros((per * channels, BLOCK), jnp.float32)
    conv = lax.fori_loop(0, me + 1, forward, start)
    back = lax.fori_loop(0, shards - me, backward, start)
    factor = 1.0 / math.sqrt(shards * tokens)
    square_row = lax.broadcasted_iota(jnp.int32, (channels, channels), 0)
    square_lane = lax.broadcasted_iota(jnp.int32, (channels, channels), 1)
    gain = jnp.sum(
        jnp.where(square_row == square_lane, jnp.broadcast_to(gain_ref[...], (channels, channels)), 0.0),
        axis=1,
        keepdims=True,
    )
    for tile in range(tiles):
        spot = slice((tile // 2) * channels, (tile // 2 + 1) * channels)
        part = slice((tile % 2) * LANES, (tile % 2 + 1) * LANES)
        lanes = slice(tile * LANES, (tile + 1) * LANES)
        own = blocks[0][tile * channels : (tile + 1) * channels, :]
        out_ref[:, lanes] = conv[spot, part] * factor + gain * own
        own = blocks[0][(tiles + tile) * channels : (tiles + tile + 1) * channels, :]
        back_ref[:, lanes] = back[spot, part] * factor + gain * own


def convolve(blocks, skip_gain, shards, channels, tokens):
    per = tokens // BLOCK
    rows = shards * per * channels
    tiles = shards * tokens // LANES
    return pl.pallas_call(
        functools.partial(convolve_kernel, shards, channels, tokens),
        out_shape=[jax.ShapeDtypeStruct((channels, tokens), jnp.float32)] * 2,
        in_specs=[pl.BlockSpec(memory_space=pltpu.VMEM)] * (shards + 1),
        out_specs=[pl.BlockSpec(memory_space=pltpu.VMEM)] * 2,
        scratch_shapes=[pltpu.VMEM((2 * rows, BLOCK), jnp.bfloat16)] * 4
        + [pltpu.VMEM((tiles, LANES), jnp.float32)]
        + [pltpu.VMEM((tiles + 1, LANES, LANES), jnp.bfloat16)] * 2,
        compiler_params=pltpu.CompilerParams(vmem_limit_bytes=KERNEL_BYTES),
        cost_estimate=pl.CostEstimate(
            flops=2 * 3 * (shards + 1) * per * per * channels * BLOCK * BLOCK,
            bytes_accessed=4 * rows * BLOCK * 2,
            transcendentals=0,
        ),
        name="convolve",
    )(*blocks, skip_gain.reshape(1, channels))


def sum_over_chan(value):
    groups = lax.axis_size("chan")
    parts = [
        lax.ppermute(value, "chan", [(i, (i + step) % groups) for i in range(groups)])
        for step in range(1, groups)
    ]
    return sum(parts, value)


def direct_body(signal, filter_taps, skip_gain, cotangent):
    shards = lax.axis_size("context")
    channels, tokens = signal.shape
    stacked = stack_local(signal, cotangent, filter_taps)
    blocks = gather_blocks(stacked, shards)
    partial_value = filter_grad(blocks, shards, channels, tokens)
    output, grad_signal = convolve(blocks, skip_gain, shards, channels, tokens)
    grad_filter = sum_over_chan(partial_value).reshape(tokens) * (1.0 / math.sqrt(shards * tokens))
    return (output, grad_signal, grad_filter)


def rotation(first, second, period):
    turned = first * second % period
    return turned.astype(jnp.float32) * (2.0 * math.pi / period)


def table_product(real_part, imag_part, cosine, sine_table):
    return (
        real_part * cosine - imag_part * sine_table,
        real_part * sine_table + imag_part * cosine,
    )


def along_last(real_part, imag_part, angle_table):
    cosine = jnp.cos(angle_table)
    sine_table = jnp.sin(angle_table)
    new_real = jnp.matmul(real_part, cosine, precision=exact_mode) - jnp.matmul(
        imag_part, sine_table, precision=exact_mode
    )
    new_imag = jnp.matmul(real_part, sine_table, precision=exact_mode) + jnp.matmul(
        imag_part, cosine, precision=exact_mode
    )
    return (new_real, new_imag)


def along_slow(real_part, imag_part, angle_table):
    cosine = jnp.cos(angle_table)
    sine_table = jnp.sin(angle_table)
    new_real = jnp.einsum("gsjd,sa->gajd", real_part, cosine, precision=exact_mode) - jnp.einsum(
        "gsjd,sa->gajd", imag_part, sine_table, precision=exact_mode
    )
    new_imag = jnp.einsum(
        "gsjd,sa->gajd", real_part, sine_table, precision=exact_mode
    ) + jnp.einsum("gsjd,sa->gajd", imag_part, cosine, precision=exact_mode)
    return (new_real, new_imag)


def finish_sections(real_part, imag_part, stride, shards, length):
    sources = jnp.arange(shards, dtype=jnp.int32)
    slower = jnp.arange(stride, dtype=jnp.int32)
    slow_angle = -rotation(slower[:, None], slower[None, :], stride)
    real_part, imag_part = along_slow(real_part, imag_part, slow_angle)
    inner_twist = -rotation(slower[:, None, None], sources[None, None, :], length)
    real_part, imag_part = table_product(
        real_part, imag_part, jnp.cos(inner_twist), jnp.sin(inner_twist)
    )
    last_angle = -rotation(sources[:, None], sources[None, :], shards)
    return along_last(real_part, imag_part, last_angle)


def forward(stacked):
    shards = lax.axis_size("context")
    position = lax.axis_index("context")
    signals, length = stacked.shape
    stride = length // shards
    period = 2 * shards * length
    sources = jnp.arange(shards, dtype=jnp.int32)
    slower = jnp.arange(stride, dtype=jnp.int32)
    blocks = stacked.reshape(signals, stride, shards)
    columns = lax.all_to_all(blocks, "context", split_axis=2, concat_axis=2, tiled=True)
    token_ids = shards * slower[:, None] + position
    order = jnp.arange(2 * shards, dtype=jnp.int32)
    first_angle = -rotation(sources[:, None], order[None, :], 2 * shards)
    real_part = jnp.matmul(columns, jnp.cos(first_angle), precision=exact_mode)
    imag_part = jnp.matmul(columns, jnp.sin(first_angle), precision=exact_mode)
    twist = -rotation(token_ids, order[None, :], period)
    real_part, imag_part = table_product(real_part, imag_part, jnp.cos(twist), jnp.sin(twist))
    spectra = jnp.stack([real_part, imag_part]).reshape(2, signals, stride, 2, shards)
    spectra = lax.all_to_all(spectra, "context", split_axis=4, concat_axis=4, tiled=True)
    real_part, imag_part = finish_sections(spectra[0], spectra[1], stride, shards, length)
    return (real_part, imag_part, order)


def inverse(real_part, imag_part, order):
    shards = lax.axis_size("context")
    position = lax.axis_index("context")
    signals, stride = (real_part.shape[0], real_part.shape[1])
    length = stride * shards
    period = 2 * shards * length
    sources = jnp.arange(shards, dtype=jnp.int32)
    slower = jnp.arange(stride, dtype=jnp.int32)
    last_angle = rotation(sources[:, None], sources[None, :], shards)
    real_part, imag_part = along_last(real_part, imag_part, last_angle)
    inner_twist = rotation(slower[:, None, None], sources[None, None, :], length)
    real_part, imag_part = table_product(
        real_part, imag_part, jnp.cos(inner_twist), jnp.sin(inner_twist)
    )
    slow_angle = rotation(slower[:, None], slower[None, :], stride)
    real_part, imag_part = along_slow(real_part, imag_part, slow_angle)
    spectra = lax.all_to_all(
        jnp.stack([real_part, imag_part]), "context", split_axis=4, concat_axis=4, tiled=True
    )
    real_part = spectra[0].reshape(signals, stride, 2 * shards)
    imag_part = spectra[1].reshape(signals, stride, 2 * shards)
    token_ids = shards * slower[:, None] + position
    twist = rotation(token_ids, order[None, :], period)
    real_part, imag_part = table_product(real_part, imag_part, jnp.cos(twist), jnp.sin(twist))
    first_angle = rotation(order[:, None], sources[None, :], 2 * shards)
    cosine = jnp.cos(first_angle)
    sine_table = jnp.sin(first_angle)
    out_real = jnp.matmul(real_part, cosine, precision=exact_mode) - jnp.matmul(
        imag_part, sine_table, precision=exact_mode
    )
    out_imag = jnp.matmul(real_part, sine_table, precision=exact_mode) + jnp.matmul(
        imag_part, cosine, precision=exact_mode
    )
    results = jnp.stack([out_real, out_imag])
    blocks = lax.all_to_all(results, "context", split_axis=3, concat_axis=3, tiled=True)
    return blocks.reshape(blocks.shape[0], signals, length)


def transform_body(signal, filter_taps, skip_gain, cotangent):
    shards = lax.axis_size("context")
    channels, length = signal.shape
    factor = 1.0 / (2 * shards * length * math.sqrt(shards * length))
    stacked = jnp.concatenate([signal, cotangent, filter_taps[None, :]], axis=0)
    real_part, imag_part, order = forward(stacked)
    sig_re = real_part[:channels]
    sig_im = imag_part[:channels]
    cot_re = real_part[channels : 2 * channels]
    cot_im = imag_part[channels : 2 * channels]
    fil_re = real_part[2 * channels :]
    fil_im = imag_part[2 * channels :]
    out_re = sig_re * fil_re - sig_im * fil_im
    out_im = sig_re * fil_im + sig_im * fil_re
    back_re = cot_re * fil_re + cot_im * fil_im
    back_im = cot_im * fil_re - cot_re * fil_im
    grad_re = jnp.sum(cot_re * sig_re + cot_im * sig_im, axis=0, keepdims=True)
    grad_im = jnp.sum(cot_im * sig_re - cot_re * sig_im, axis=0, keepdims=True)
    restored = inverse(
        jnp.concatenate([out_re - back_im, grad_re], axis=0),
        jnp.concatenate([out_im + back_re, grad_im], axis=0),
        order,
    )
    conv_out = restored[0, :channels]
    conv_back = restored[1, :channels]
    partial_value = restored[0, channels]
    output = conv_out * factor + skip_gain[:, None] * signal
    grad_signal = conv_back * factor + skip_gain[:, None] * cotangent
    grad_filter = lax.psum(partial_value * factor, "chan")
    return (output, grad_signal, grad_filter)


def fits_direct(channels, tokens, shards):
    held = 4 * shards * tokens * (2 * channels + 1)
    scratch = 16 * shards * tokens * channels + 4 * (shards * tokens + LANES) * LANES
    whole = channels % PACKED_ROWS == 0 and tokens % (8 * LANES) == 0 and shards & (shards - 1) == 0
    return whole and shards > 1 and 2 * held + scratch < KERNEL_BYTES // 2


def body(signal, filter_taps, skip_gain, cotangent):
    channels, tokens = signal.shape
    if fits_direct(channels, tokens, lax.axis_size("context")):
        return direct_body(signal, filter_taps, skip_gain, cotangent)
    return transform_body(signal, filter_taps, skip_gain, cotangent)


def solution(mesh):
    return jax.shard_map(
        body,
        mesh=mesh,
        in_specs=(P("chan", "context"), P("context"), P("chan"), P("chan", "context")),
        out_specs=(P("chan", "context"), P("chan", "context"), P("context")),
        check_vma=False,
    )
```

```python
import functools
import math

import jax
import jax.numpy as jnp
from jax import lax
from jax.experimental import pallas as pl
from jax.experimental.pallas import tpu as pltpu
from jax.sharding import PartitionSpec as P

exact_mode = lax.Precision.HIGHEST

LANES = 128
BLOCK = 256
PACKED_ROWS = 16
KERNEL_BYTES = 48 * 1024 * 1024


def halves(value):
    high = value.astype(jnp.bfloat16)
    low = (value - high.astype(jnp.float32)).astype(jnp.bfloat16)
    return high, low


def dot(left, right, left_dim, right_dim):
    return lax.dot_general(
        left, right, (((left_dim,), (right_dim,)), ((), ())), preferred_element_type=jnp.float32
    )


def dot_halves(left, right, left_dim, right_dim):
    return (
        dot(left[0], right[0], left_dim, right_dim)
        + dot(left[0], right[1], left_dim, right_dim)
        + dot(left[1], right[0], left_dim, right_dim)
    )


def stack_kernel(signal_ref, cotangent_ref, taps_ref, out_ref):
    channels, tokens = signal_ref.shape
    row = 0
    for source in (signal_ref, cotangent_ref):
        for tile in range(tokens // LANES):
            out_ref[row : row + channels, :] = source[:, tile * LANES : (tile + 1) * LANES]
            row += channels
    out_ref[row:, :] = taps_ref[...]


def stack_local(signal, cotangent, taps):
    channels, tokens = signal.shape
    rows = (2 * channels * tokens + tokens) // LANES
    return pl.pallas_call(
        stack_kernel,
        out_shape=pltpu.VMEM((rows, LANES), jnp.float32),
        in_specs=[pl.BlockSpec(memory_space=pltpu.VMEM)] * 3,
        out_specs=pl.BlockSpec(memory_space=pltpu.VMEM),
        name="stack_local",
    )(signal, cotangent, taps.reshape(tokens // LANES, LANES))


def gather_blocks(stacked, shards):
    def flipped(value, bits):
        return lax.ppermute(value, "context", [(i, i ^ bits) for i in range(shards)])

    found = {0: stacked}
    for bits in range(2, shards, 2):
        found[bits] = flipped(stacked, bits)
    for bits in range(0, shards, 2):
        found[bits + 1] = flipped(found[bits], 1)
    return [found[bits] for bits in range(shards)]


def place_rows(block_ref, index, channels, tokens, first, high_ref, low_ref, start):
    per = tokens // BLOCK
    for tile in range(tokens // LANES):
        rows = first + tile * channels
        high, low = halves(block_ref[rows : rows + channels, :])
        at = pl.multiple_of((index * per + tile // 2) * channels + start, PACKED_ROWS)
        lanes = slice((tile % 2) * LANES, (tile % 2 + 1) * LANES)
        high_ref[pl.ds(at, channels), lanes] = high
        low_ref[pl.ds(at, channels), lanes] = low


def filter_grad_kernel(shards, channels, tokens, *refs):
    blocks, out_ref = refs[:shards], refs[shards]
    sig_high, sig_low, cot_high, cot_low, folded = refs[shards + 1 :]
    me = lax.axis_index("context")
    per = tokens // BLOCK
    rows = shards * per * channels
    cot_high[rows:, :] = jnp.zeros((rows, BLOCK), jnp.bfloat16)
    cot_low[rows:, :] = jnp.zeros((rows, BLOCK), jnp.bfloat16)
    for bits in range(shards):
        index = me ^ bits
        place_rows(blocks[bits], index, channels, tokens, 0, sig_high, sig_low, 0)
        place_rows(
            blocks[bits], index, channels, tokens, channels * tokens // LANES, cot_high, cot_low, 0
        )
    sig = (sig_high[...], sig_low[...])
    for lag in range(per + 1):
        at = pl.multiple_of((me * per + lag) * channels, PACKED_ROWS)
        window = (cot_high[pl.ds(at, rows), :], cot_low[pl.ds(at, rows), :])
        folded[:, lag * BLOCK : (lag + 1) * BLOCK] = dot_halves(sig, window, 0, 0)
    width = (per + 1) * BLOCK - LANES
    total = None
    for group in range(LANES // 8):
        part = (
            folded[8 * group : 8 * group + 8, :width]
            + folded[LANES + 8 * group : LANES + 8 * group + 8, LANES:]
        )
        if group:
            part = pltpu.roll(part, width - 8 * group, 1)
        total = part if total is None else total + part
    row = lax.broadcasted_iota(jnp.int32, total.shape, 0)
    for step in (1, 2, 4):
        total = jnp.where((row & step) != 0, pltpu.roll(total, width - step, 1), total)
    out_ref[...] = jnp.sum(total, axis=0, keepdims=True)[:, :tokens]


def filter_grad(blocks, shards, channels, tokens):
    rows = shards * tokens // BLOCK * channels
    per = tokens // BLOCK
    return pl.pallas_call(
        functools.partial(filter_grad_kernel, shards, channels, tokens),
        out_shape=jax.ShapeDtypeStruct((1, tokens), jnp.float32),
        in_specs=[pl.BlockSpec(memory_space=pltpu.VMEM)] * shards,
        out_specs=pl.BlockSpec(memory_space=pltpu.VMEM),
        scratch_shapes=[
            pltpu.VMEM((rows, BLOCK), jnp.bfloat16),
            pltpu.VMEM((rows, BLOCK), jnp.bfloat16),
            pltpu.VMEM((2 * rows, BLOCK), jnp.bfloat16),
            pltpu.VMEM((2 * rows, BLOCK), jnp.bfloat16),
            pltpu.VMEM((BLOCK, (per + 1) * BLOCK), jnp.float32),
        ],
        compiler_params=pltpu.CompilerParams(vmem_limit_bytes=KERNEL_BYTES),
        cost_estimate=pl.CostEstimate(
            flops=2 * 3 * (per + 1) * rows * BLOCK * BLOCK, bytes_accessed=4 * rows * BLOCK * 2, transcendentals=0
        ),
        name="filter_grad",
    )(*blocks)


def toeplitz_kernel(shards, channels, tokens, *refs):
    blocks, high_ref, low_ref, taps = refs[:shards], *refs[shards:]
    me = lax.axis_index("context")
    tiles = tokens // LANES
    first = 2 * channels * tiles
    taps[0] = jnp.zeros((tiles, LANES), jnp.float32)
    for bits in range(shards):
        taps[(me ^ bits) + 1] = blocks[bits][first : first + tiles, :]
    high_ref[0] = jnp.zeros((LANES, LANES), jnp.bfloat16)
    low_ref[0] = jnp.zeros((LANES, LANES), jnp.bfloat16)
    width = (tiles + 1) * LANES
    row = lax.broadcasted_iota(jnp.int32, (8, width), 0)

    def build(step, carry):
        last, sheet = taps[step], taps[step + 1]
        lines = [last[tiles - 1 : tiles, :]] + [sheet[n : n + 1, :] for n in range(tiles)]
        skewed = jnp.concatenate([jnp.broadcast_to(line, (8, LANES)) for line in lines], axis=1)
        for bit in (1, 2, 4):
            skewed = jnp.where((row & bit) != 0, pltpu.roll(skewed, bit, 1), skewed)
        for group in range(LANES // PACKED_ROWS):
            top, bottom = (
                pltpu.roll(skewed, PACKED_ROWS * group + rows, 1) if group + rows else skewed
                for rows in (0, 8)
            )
            pair = halves(jnp.concatenate([top, bottom], axis=0))
            for ref, part in zip((high_ref, low_ref), pair):
                for tile in range(tiles):
                    ref[
                        step * tiles + tile + 1, group * PACKED_ROWS : (group + 1) * PACKED_ROWS, :
                    ] = part[:, (tile + 1) * LANES : (tile + 2) * LANES]
        return carry

    lax.fori_loop(0, shards, build, 0)


def toeplitz_tiles(blocks, shards, channels, tokens):
    tiles = tokens // LANES
    shape = (shards * tiles + 1, LANES, LANES)
    return pl.pallas_call(
        functools.partial(toeplitz_kernel, shards, channels, tokens),
        out_shape=[pltpu.VMEM(shape, jnp.bfloat16)] * 2,
        in_specs=[pl.BlockSpec(memory_space=pltpu.VMEM)] * shards,
        out_specs=[pl.BlockSpec(memory_space=pltpu.VMEM)] * 2,
        scratch_shapes=[pltpu.VMEM((shards + 1, tiles, LANES), jnp.float32)],
        compiler_params=pltpu.CompilerParams(vmem_limit_bytes=KERNEL_BYTES),
        cost_estimate=pl.CostEstimate(
            flops=16 * shape[0] * LANES * LANES, bytes_accessed=4 * shape[0] * LANES * LANES, transcendentals=0
        ),
        name="toeplitz_tiles",
    )(*blocks)


def place_stacked(block_ref, index, channels, tokens, first, ref, start):
    for tile in range(tokens // LANES):
        rows = first + tile * channels
        both = jnp.concatenate(halves(block_ref[rows : rows + channels, :]), axis=0)
        at = pl.multiple_of((index * (tokens // LANES) + tile) * 2 * channels + start, PACKED_ROWS)
        ref[pl.ds(at, 2 * channels), :] = both


def convolve_kernel(shards, channels, tokens, *refs):
    blocks, toe_high, toe_low, gain_ref = refs[:shards], *refs[shards : shards + 3]
    out_ref, back_ref, sig, cot = refs[shards + 3 :]
    me = lax.axis_index("context")
    tiles = tokens // LANES
    rows = 2 * shards * tiles * channels
    sig[:rows, :] = jnp.zeros((rows, LANES), jnp.bfloat16)
    cot[rows:, :] = jnp.zeros((rows, LANES), jnp.bfloat16)
    for bits in range(shards):
        index = me ^ bits
        place_stacked(blocks[bits], index, channels, tokens, 0, sig, rows)
        place_stacked(blocks[bits], index, channels, tokens, channels * tiles, cot, 0)
    count = 2 * tiles * channels

    def window(ref, tile):
        return ref[pl.ds(pl.multiple_of(tile * 2 * channels, PACKED_ROWS), count), :]

    def forward(trip, total):
        lags = [trip * tiles + n for n in range(tiles)]
        left = jnp.concatenate([window(sig, (shards + me) * tiles - lag) for lag in lags], axis=1)
        right = jnp.concatenate(
            [jnp.concatenate([toe_high[lag + 1], toe_low[lag + 1]], axis=1) for lag in lags], axis=0
        )
        return total + dot(left, right, 1, 0)

    def backward(trip, total):
        lags = [trip * tiles + n for n in range(tiles)]
        left = jnp.concatenate([window(cot, me * tiles + lag) for lag in lags], axis=1)
        right = jnp.concatenate(
            [jnp.concatenate([toe_high[lag + 1], toe_low[lag + 1]], axis=0) for lag in lags], axis=1
        )
        return total + dot(left, right, 1, 1)

    start = jnp.zeros((count, 2 * LANES), jnp.float32)
    conv = lax.fori_loop(0, me + 1, forward, start)
    back = lax.fori_loop(0, shards - me, backward, start)
    factor = 1.0 / math.sqrt(shards * tokens)
    square_row = lax.broadcasted_iota(jnp.int32, (channels, channels), 0)
    square_lane = lax.broadcasted_iota(jnp.int32, (channels, channels), 1)
    gain = jnp.sum(
        jnp.where(square_row == square_lane, jnp.broadcast_to(gain_ref[...], (channels, channels)), 0.0),
        axis=1,
        keepdims=True,
    )
    for tile in range(tiles):
        lanes = slice(tile * LANES, (tile + 1) * LANES)
        for ref, value, first in ((out_ref, conv, 0), (back_ref, back, tiles)):
            own = blocks[0][(first + tile) * channels : (first + tile + 1) * channels, :]
            quarters = value[tile * 2 * channels : (tile + 1) * 2 * channels, :]
            both = quarters[:channels, :] + quarters[channels:, :]
            ref[:, lanes] = (both[:, :LANES] + both[:, LANES:]) * factor + gain * own


def convolve(blocks, toeplitz, skip_gain, shards, channels, tokens):
    per = tokens // BLOCK
    rows = shards * per * channels
    return pl.pallas_call(
        functools.partial(convolve_kernel, shards, channels, tokens),
        out_shape=[jax.ShapeDtypeStruct((channels, tokens), jnp.float32)] * 2,
        in_specs=[pl.BlockSpec(memory_space=pltpu.VMEM)] * (shards + 3),
        out_specs=[pl.BlockSpec(memory_space=pltpu.VMEM)] * 2,
        scratch_shapes=[pltpu.VMEM((8 * rows, LANES), jnp.bfloat16)] * 2,
        compiler_params=pltpu.CompilerParams(vmem_limit_bytes=KERNEL_BYTES),
        cost_estimate=pl.CostEstimate(
            flops=2 * 4 * (shards + 1) * per * per * channels * BLOCK * BLOCK,
            bytes_accessed=4 * rows * BLOCK * 2,
            transcendentals=0,
        ),
        name="convolve",
    )(*blocks, *toeplitz, skip_gain.reshape(1, channels))


def direct_body(signal, filter_taps, skip_gain, cotangent):
    shards, groups = lax.axis_size("context"), lax.axis_size("chan")
    channels, tokens = signal.shape
    stacked = stack_local(signal, cotangent, filter_taps)
    blocks = gather_blocks(stacked, shards)
    value = filter_grad(blocks, shards, channels, tokens)
    toeplitz = toeplitz_tiles(blocks, shards, channels, tokens)
    bits = 1
    while bits < groups:
        value = value + lax.ppermute(value, "chan", [(i, i ^ bits) for i in range(groups)])
        if bits == 1:
            value, *toeplitz = lax.optimization_barrier((value, *toeplitz))
        bits *= 2
    output, grad_signal = convolve(blocks, toeplitz, skip_gain, shards, channels, tokens)
    grad_filter = value.reshape(tokens) * (1.0 / math.sqrt(shards * tokens))
    return (output, grad_signal, grad_filter)


def rotation(first, second, period):
    turned = first * second % period
    return turned.astype(jnp.float32) * (2.0 * math.pi / period)


def table_product(real_part, imag_part, cosine, sine_table):
    return (
        real_part * cosine - imag_part * sine_table,
        real_part * sine_table + imag_part * cosine,
    )


def along_last(real_part, imag_part, angle_table):
    cosine = jnp.cos(angle_table)
    sine_table = jnp.sin(angle_table)
    new_real = jnp.matmul(real_part, cosine, precision=exact_mode) - jnp.matmul(
        imag_part, sine_table, precision=exact_mode
    )
    new_imag = jnp.matmul(real_part, sine_table, precision=exact_mode) + jnp.matmul(
        imag_part, cosine, precision=exact_mode
    )
    return (new_real, new_imag)


def along_slow(real_part, imag_part, angle_table):
    cosine = jnp.cos(angle_table)
    sine_table = jnp.sin(angle_table)
    new_real = jnp.einsum("gsjd,sa->gajd", real_part, cosine, precision=exact_mode) - jnp.einsum(
        "gsjd,sa->gajd", imag_part, sine_table, precision=exact_mode
    )
    new_imag = jnp.einsum(
        "gsjd,sa->gajd", real_part, sine_table, precision=exact_mode
    ) + jnp.einsum("gsjd,sa->gajd", imag_part, cosine, precision=exact_mode)
    return (new_real, new_imag)


def finish_sections(real_part, imag_part, stride, shards, length):
    sources = jnp.arange(shards, dtype=jnp.int32)
    slower = jnp.arange(stride, dtype=jnp.int32)
    slow_angle = -rotation(slower[:, None], slower[None, :], stride)
    real_part, imag_part = along_slow(real_part, imag_part, slow_angle)
    inner_twist = -rotation(slower[:, None, None], sources[None, None, :], length)
    real_part, imag_part = table_product(
        real_part, imag_part, jnp.cos(inner_twist), jnp.sin(inner_twist)
    )
    last_angle = -rotation(sources[:, None], sources[None, :], shards)
    return along_last(real_part, imag_part, last_angle)


def forward(stacked):
    shards = lax.axis_size("context")
    position = lax.axis_index("context")
    signals, length = stacked.shape
    stride = length // shards
    period = 2 * shards * length
    sources = jnp.arange(shards, dtype=jnp.int32)
    slower = jnp.arange(stride, dtype=jnp.int32)
    blocks = stacked.reshape(signals, stride, shards)
    columns = lax.all_to_all(blocks, "context", split_axis=2, concat_axis=2, tiled=True)
    token_ids = shards * slower[:, None] + position
    order = jnp.arange(2 * shards, dtype=jnp.int32)
    first_angle = -rotation(sources[:, None], order[None, :], 2 * shards)
    real_part = jnp.matmul(columns, jnp.cos(first_angle), precision=exact_mode)
    imag_part = jnp.matmul(columns, jnp.sin(first_angle), precision=exact_mode)
    twist = -rotation(token_ids, order[None, :], period)
    real_part, imag_part = table_product(real_part, imag_part, jnp.cos(twist), jnp.sin(twist))
    spectra = jnp.stack([real_part, imag_part]).reshape(2, signals, stride, 2, shards)
    spectra = lax.all_to_all(spectra, "context", split_axis=4, concat_axis=4, tiled=True)
    real_part, imag_part = finish_sections(spectra[0], spectra[1], stride, shards, length)
    return (real_part, imag_part, order)


def inverse(real_part, imag_part, order):
    shards = lax.axis_size("context")
    position = lax.axis_index("context")
    signals, stride = (real_part.shape[0], real_part.shape[1])
    length = stride * shards
    period = 2 * shards * length
    sources = jnp.arange(shards, dtype=jnp.int32)
    slower = jnp.arange(stride, dtype=jnp.int32)
    last_angle = rotation(sources[:, None], sources[None, :], shards)
    real_part, imag_part = along_last(real_part, imag_part, last_angle)
    inner_twist = rotation(slower[:, None, None], sources[None, None, :], length)
    real_part, imag_part = table_product(
        real_part, imag_part, jnp.cos(inner_twist), jnp.sin(inner_twist)
    )
    slow_angle = rotation(slower[:, None], slower[None, :], stride)
    real_part, imag_part = along_slow(real_part, imag_part, slow_angle)
    spectra = lax.all_to_all(
        jnp.stack([real_part, imag_part]), "context", split_axis=4, concat_axis=4, tiled=True
    )
    real_part = spectra[0].reshape(signals, stride, 2 * shards)
    imag_part = spectra[1].reshape(signals, stride, 2 * shards)
    token_ids = shards * slower[:, None] + position
    twist = rotation(token_ids, order[None, :], period)
    real_part, imag_part = table_product(real_part, imag_part, jnp.cos(twist), jnp.sin(twist))
    first_angle = rotation(order[:, None], sources[None, :], 2 * shards)
    cosine = jnp.cos(first_angle)
    sine_table = jnp.sin(first_angle)
    out_real = jnp.matmul(real_part, cosine, precision=exact_mode) - jnp.matmul(
        imag_part, sine_table, precision=exact_mode
    )
    out_imag = jnp.matmul(real_part, sine_table, precision=exact_mode) + jnp.matmul(
        imag_part, cosine, precision=exact_mode
    )
    results = jnp.stack([out_real, out_imag])
    blocks = lax.all_to_all(results, "context", split_axis=3, concat_axis=3, tiled=True)
    return blocks.reshape(blocks.shape[0], signals, length)


def transform_body(signal, filter_taps, skip_gain, cotangent):
    shards = lax.axis_size("context")
    channels, length = signal.shape
    factor = 1.0 / (2 * shards * length * math.sqrt(shards * length))
    stacked = jnp.concatenate([signal, cotangent, filter_taps[None, :]], axis=0)
    real_part, imag_part, order = forward(stacked)
    sig_re = real_part[:channels]
    sig_im = imag_part[:channels]
    cot_re = real_part[channels : 2 * channels]
    cot_im = imag_part[channels : 2 * channels]
    fil_re = real_part[2 * channels :]
    fil_im = imag_part[2 * channels :]
    out_re = sig_re * fil_re - sig_im * fil_im
    out_im = sig_re * fil_im + sig_im * fil_re
    back_re = cot_re * fil_re + cot_im * fil_im
    back_im = cot_im * fil_re - cot_re * fil_im
    grad_re = jnp.sum(cot_re * sig_re + cot_im * sig_im, axis=0, keepdims=True)
    grad_im = jnp.sum(cot_im * sig_re - cot_re * sig_im, axis=0, keepdims=True)
    restored = inverse(
        jnp.concatenate([out_re - back_im, grad_re], axis=0),
        jnp.concatenate([out_im + back_re, grad_im], axis=0),
        order,
    )
    conv_out = restored[0, :channels]
    conv_back = restored[1, :channels]
    partial_value = restored[0, channels]
    output = conv_out * factor + skip_gain[:, None] * signal
    grad_signal = conv_back * factor + skip_gain[:, None] * cotangent
    grad_filter = lax.psum(partial_value * factor, "chan")
    return (output, grad_signal, grad_filter)


def fits_direct(channels, tokens, shards):
    held = 4 * shards * tokens * (2 * channels + 1)
    scratch = 16 * shards * tokens * channels + 4 * (shards * tokens + LANES) * LANES
    groups = lax.axis_size("chan")
    whole = groups & (groups - 1) == 0 and channels % PACKED_ROWS == 0 and tokens % (8 * LANES) == 0 and shards & (shards - 1) == 0
    return whole and shards > 1 and 2 * held + scratch < KERNEL_BYTES // 2


def body(signal, filter_taps, skip_gain, cotangent):
    channels, tokens = signal.shape
    if fits_direct(channels, tokens, lax.axis_size("context")):
        return direct_body(signal, filter_taps, skip_gain, cotangent)
    return transform_body(signal, filter_taps, skip_gain, cotangent)


def solution(mesh):
    return jax.shard_map(
        body,
        mesh=mesh,
        in_specs=(P("chan", "context"), P("context"), P("chan"), P("chan", "context")),
        out_specs=(P("chan", "context"), P("chan", "context"), P("context")),
        check_vma=False,
    )
```

```python
import functools
import math

import jax
import jax.numpy as jnp
from jax import lax
from jax.experimental import pallas as pl
from jax.experimental.pallas import tpu as pltpu
from jax.sharding import PartitionSpec as P

exact_mode = lax.Precision.HIGHEST

LANES = 128
BLOCK = 256
PACKED_ROWS = 16
KERNEL_BYTES = 48 * 1024 * 1024


def halves(value):
    high = value.astype(jnp.bfloat16)
    low = (value - high.astype(jnp.float32)).astype(jnp.bfloat16)
    return high, low


def dot(left, right, left_dim, right_dim):
    return lax.dot_general(
        left, right, (((left_dim,), (right_dim,)), ((), ())), preferred_element_type=jnp.float32
    )


def dot_halves(left, right, left_dim, right_dim):
    return (
        dot(left[0], right[0], left_dim, right_dim)
        + dot(left[0], right[1], left_dim, right_dim)
        + dot(left[1], right[0], left_dim, right_dim)
    )


def stack_kernel(signal_ref, cotangent_ref, taps_ref, out_ref):
    channels, tokens = signal_ref.shape
    row = 0
    for source in (signal_ref, cotangent_ref):
        for tile in range(tokens // LANES):
            out_ref[row : row + channels, :] = source[:, tile * LANES : (tile + 1) * LANES]
            row += channels
    out_ref[row:, :] = taps_ref[...]


def stack_local(signal, cotangent, taps):
    channels, tokens = signal.shape
    rows = (2 * channels * tokens + tokens) // LANES
    return pl.pallas_call(
        stack_kernel,
        out_shape=pltpu.VMEM((rows, LANES), jnp.float32),
        in_specs=[pl.BlockSpec(memory_space=pltpu.VMEM)] * 3,
        out_specs=pl.BlockSpec(memory_space=pltpu.VMEM),
        name="stack_local",
    )(signal, cotangent, taps.reshape(tokens // LANES, LANES))


def gather_blocks(stacked, shards):
    def flipped(value, bits):
        return lax.ppermute(value, "context", [(i, i ^ bits) for i in range(shards)])

    found = {0: stacked}
    for bits in range(2, shards, 2):
        found[bits] = flipped(stacked, bits)
    for bits in range(0, shards, 2):
        found[bits + 1] = flipped(found[bits], 1)
    return [found[bits] for bits in range(shards)]


def place_rows(block_ref, index, channels, tokens, first, high_ref, low_ref, start):
    per = tokens // BLOCK
    for tile in range(tokens // LANES):
        rows = first + tile * channels
        high, low = halves(block_ref[rows : rows + channels, :])
        at = pl.multiple_of((index * per + tile // 2) * channels + start, PACKED_ROWS)
        lanes = slice((tile % 2) * LANES, (tile % 2 + 1) * LANES)
        high_ref[pl.ds(at, channels), lanes] = high
        low_ref[pl.ds(at, channels), lanes] = low


def filter_grad_kernel(shards, channels, tokens, *refs):
    blocks, out_ref = refs[:shards], refs[shards]
    sig_high, sig_low, cot_high, cot_low, folded = refs[shards + 1 :]
    me = lax.axis_index("context")
    per = tokens // BLOCK
    rows = shards * per * channels
    cot_high[rows:, :] = jnp.zeros((rows, BLOCK), jnp.bfloat16)
    cot_low[rows:, :] = jnp.zeros((rows, BLOCK), jnp.bfloat16)
    for bits in range(shards):
        index = me ^ bits
        place_rows(blocks[bits], index, channels, tokens, 0, sig_high, sig_low, 0)
        place_rows(
            blocks[bits], index, channels, tokens, channels * tokens // LANES, cot_high, cot_low, 0
        )
    sig = (sig_high[...], sig_low[...])
    for lag in range(per + 1):
        at = pl.multiple_of((me * per + lag) * channels, PACKED_ROWS)
        window = (cot_high[pl.ds(at, rows), :], cot_low[pl.ds(at, rows), :])
        folded[:, lag * BLOCK : (lag + 1) * BLOCK] = dot_halves(sig, window, 0, 0)
    width = (per + 1) * BLOCK - LANES
    total = None
    for group in range(LANES // 8):
        part = (
            folded[8 * group : 8 * group + 8, :width]
            + folded[LANES + 8 * group : LANES + 8 * group + 8, LANES:]
        )
        if group:
            part = pltpu.roll(part, width - 8 * group, 1)
        total = part if total is None else total + part
    row = lax.broadcasted_iota(jnp.int32, total.shape, 0)
    for step in (1, 2, 4):
        total = jnp.where((row & step) != 0, pltpu.roll(total, width - step, 1), total)
    out_ref[...] = jnp.sum(total, axis=0, keepdims=True)[:, :tokens]


def filter_grad(blocks, shards, channels, tokens):
    rows = shards * tokens // BLOCK * channels
    per = tokens // BLOCK
    return pl.pallas_call(
        functools.partial(filter_grad_kernel, shards, channels, tokens),
        out_shape=jax.ShapeDtypeStruct((1, tokens), jnp.float32),
        in_specs=[pl.BlockSpec(memory_space=pltpu.VMEM)] * shards,
        out_specs=pl.BlockSpec(memory_space=pltpu.VMEM),
        scratch_shapes=[
            pltpu.VMEM((rows, BLOCK), jnp.bfloat16),
            pltpu.VMEM((rows, BLOCK), jnp.bfloat16),
            pltpu.VMEM((2 * rows, BLOCK), jnp.bfloat16),
            pltpu.VMEM((2 * rows, BLOCK), jnp.bfloat16),
            pltpu.VMEM((BLOCK, (per + 1) * BLOCK), jnp.float32),
        ],
        compiler_params=pltpu.CompilerParams(vmem_limit_bytes=KERNEL_BYTES),
        cost_estimate=pl.CostEstimate(
            flops=2 * 3 * (per + 1) * rows * BLOCK * BLOCK, bytes_accessed=4 * rows * BLOCK * 2, transcendentals=0
        ),
        name="filter_grad",
    )(*blocks)


def toeplitz_kernel(shards, channels, tokens, *refs):
    blocks, high_ref, low_ref, taps, skew = refs[:shards], *refs[shards:]
    me = lax.axis_index("context")
    tiles = tokens // LANES
    first = 2 * channels * tiles
    taps[0] = jnp.zeros((tiles, LANES), jnp.float32)
    for bits in range(shards):
        taps[(me ^ bits) + 1] = blocks[bits][first : first + tiles, :]
    high_ref[0] = jnp.zeros((LANES, LANES), jnp.bfloat16)
    low_ref[0] = jnp.zeros((LANES, LANES), jnp.bfloat16)
    width = (tiles + 1) * LANES

    for step in range(shards):
        last, sheet = taps[step], taps[step + 1]
        lines = [last[tiles - 1 : tiles, :]] + [sheet[n : n + 1, :] for n in range(tiles)]
        lean = jnp.concatenate([jnp.broadcast_to(line, (8, LANES)) for line in lines], axis=1)
        lean = pltpu.roll(lean, 0, 1, stride=1, stride_axis=0)
        skew[step] = lean

    def build(step, carry):
        skewed = skew[step]
        for group in range(LANES // PACKED_ROWS):
            top, bottom = (
                pltpu.roll(skewed, PACKED_ROWS * group + rows, 1) if group + rows else skewed
                for rows in (0, 8)
            )
            pair = halves(jnp.concatenate([top, bottom], axis=0))
            for ref, part in zip((high_ref, low_ref), pair):
                for tile in range(tiles):
                    ref[
                        step * tiles + tile + 1, group * PACKED_ROWS : (group + 1) * PACKED_ROWS, :
                    ] = part[:, (tile + 1) * LANES : (tile + 2) * LANES]
        return carry

    lax.fori_loop(0, shards, build, 0, unroll=min(4, shards))


def toeplitz_tiles(blocks, shards, channels, tokens):
    tiles = tokens // LANES
    shape = (shards * tiles + 1, LANES, LANES)
    return pl.pallas_call(
        functools.partial(toeplitz_kernel, shards, channels, tokens),
        out_shape=[pltpu.VMEM(shape, jnp.bfloat16)] * 2,
        in_specs=[pl.BlockSpec(memory_space=pltpu.VMEM)] * shards,
        out_specs=[pl.BlockSpec(memory_space=pltpu.VMEM)] * 2,
        scratch_shapes=[pltpu.VMEM((shards + 1, tiles, LANES), jnp.float32), pltpu.VMEM((shards, 8, (tiles + 1) * LANES), jnp.float32)],
        compiler_params=pltpu.CompilerParams(vmem_limit_bytes=KERNEL_BYTES),
        cost_estimate=pl.CostEstimate(
            flops=16 * shape[0] * LANES * LANES, bytes_accessed=4 * shape[0] * LANES * LANES, transcendentals=0
        ),
        name="toeplitz_tiles",
    )(*blocks)


def place_stacked(block_ref, index, channels, tokens, first, ref, start):
    for tile in range(tokens // LANES):
        rows = first + tile * channels
        both = jnp.concatenate(halves(block_ref[rows : rows + channels, :]), axis=0)
        at = pl.multiple_of((index * (tokens // LANES) + tile) * 2 * channels + start, PACKED_ROWS)
        ref[pl.ds(at, 2 * channels), :] = both


def convolve_kernel(shards, channels, tokens, *refs):
    blocks, toe_high, toe_low, gain_ref = refs[:shards], *refs[shards : shards + 3]
    out_ref, back_ref, sig, cot = refs[shards + 3 :]
    me = lax.axis_index("context")
    tiles = tokens // LANES
    rows = 2 * shards * tiles * channels
    sig[:rows, :] = jnp.zeros((rows, LANES), jnp.bfloat16)
    cot[rows:, :] = jnp.zeros((rows, LANES), jnp.bfloat16)
    for bits in range(shards):
        index = me ^ bits
        place_stacked(blocks[bits], index, channels, tokens, 0, sig, rows)
        place_stacked(blocks[bits], index, channels, tokens, channels * tiles, cot, 0)
    count = 2 * tiles * channels

    def window(ref, tile):
        return ref[pl.ds(pl.multiple_of(tile * 2 * channels, PACKED_ROWS), count), :]

    def forward(trip, total):
        for part in range(2):
            lags = [(trip * 2 + part) * tiles + n for n in range(tiles)]
            left = jnp.concatenate([window(sig, (shards + me) * tiles - lag) for lag in lags], axis=1)
            right = jnp.concatenate(
                [jnp.concatenate([toe_high[lag + 1], toe_low[lag + 1]], axis=1) for lag in lags], axis=0
            )
            total = total + dot(left, right, 1, 0)
        return total

    def backward(trip, total):
        for part in range(2):
            lags = [(trip * 2 + part) * tiles + n for n in range(tiles)]
            left = jnp.concatenate([window(cot, me * tiles + lag) for lag in lags], axis=1)
            right = jnp.concatenate(
                [jnp.concatenate([toe_high[lag + 1], toe_low[lag + 1]], axis=0) for lag in lags], axis=1
            )
            total = total + dot(left, right, 1, 1)
        return total

    start = jnp.zeros((count, 2 * LANES), jnp.float32)
    conv = lax.fori_loop(0, me // 2 + 1, forward, start)
    back = lax.fori_loop(0, (shards - me + 1) // 2, backward, start)
    factor = 1.0 / math.sqrt(shards * tokens)
    square_row = lax.broadcasted_iota(jnp.int32, (channels, channels), 0)
    square_lane = lax.broadcasted_iota(jnp.int32, (channels, channels), 1)
    gain = jnp.sum(
        jnp.where(square_row == square_lane, jnp.broadcast_to(gain_ref[...], (channels, channels)), 0.0),
        axis=1,
        keepdims=True,
    )
    for tile in range(tiles):
        lanes = slice(tile * LANES, (tile + 1) * LANES)
        for ref, value, first in ((out_ref, conv, 0), (back_ref, back, tiles)):
            own = blocks[0][(first + tile) * channels : (first + tile + 1) * channels, :]
            quarters = value[tile * 2 * channels : (tile + 1) * 2 * channels, :]
            both = quarters[:channels, :] + quarters[channels:, :]
            ref[:, lanes] = (both[:, :LANES] + both[:, LANES:]) * factor + gain * own


def convolve(blocks, toeplitz, skip_gain, shards, channels, tokens):
    per = tokens // BLOCK
    rows = shards * per * channels
    return pl.pallas_call(
        functools.partial(convolve_kernel, shards, channels, tokens),
        out_shape=[jax.ShapeDtypeStruct((channels, tokens), jnp.float32)] * 2,
        in_specs=[pl.BlockSpec(memory_space=pltpu.VMEM)] * (shards + 3),
        out_specs=[pl.BlockSpec(memory_space=pltpu.VMEM)] * 2,
        scratch_shapes=[pltpu.VMEM((8 * rows, LANES), jnp.bfloat16)] * 2,
        compiler_params=pltpu.CompilerParams(vmem_limit_bytes=KERNEL_BYTES),
        cost_estimate=pl.CostEstimate(
            flops=2 * 4 * (shards + 1) * per * per * channels * BLOCK * BLOCK,
            bytes_accessed=4 * rows * BLOCK * 2,
            transcendentals=0,
        ),
        name="convolve",
    )(*blocks, *toeplitz, skip_gain.reshape(1, channels))


def direct_body(signal, filter_taps, skip_gain, cotangent):
    shards, groups = lax.axis_size("context"), lax.axis_size("chan")
    channels, tokens = signal.shape
    stacked = stack_local(signal, cotangent, filter_taps)
    blocks = gather_blocks(stacked, shards)
    value = filter_grad(blocks, shards, channels, tokens)
    toeplitz = toeplitz_tiles(blocks, shards, channels, tokens)
    bits = 1
    while bits < groups:
        value = value + lax.ppermute(value, "chan", [(i, i ^ bits) for i in range(groups)])
        if bits == 1:
            value, *toeplitz = lax.optimization_barrier((value, *toeplitz))
        bits *= 2
    output, grad_signal = convolve(blocks, toeplitz, skip_gain, shards, channels, tokens)
    grad_filter = value.reshape(tokens) * (1.0 / math.sqrt(shards * tokens))
    return (output, grad_signal, grad_filter)


def rotation(first, second, period):
    turned = first * second % period
    return turned.astype(jnp.float32) * (2.0 * math.pi / period)


def table_product(real_part, imag_part, cosine, sine_table):
    return (
        real_part * cosine - imag_part * sine_table,
        real_part * sine_table + imag_part * cosine,
    )


def along_last(real_part, imag_part, angle_table):
    cosine = jnp.cos(angle_table)
    sine_table = jnp.sin(angle_table)
    new_real = jnp.matmul(real_part, cosine, precision=exact_mode) - jnp.matmul(
        imag_part, sine_table, precision=exact_mode
    )
    new_imag = jnp.matmul(real_part, sine_table, precision=exact_mode) + jnp.matmul(
        imag_part, cosine, precision=exact_mode
    )
    return (new_real, new_imag)


def along_slow(real_part, imag_part, angle_table):
    cosine = jnp.cos(angle_table)
    sine_table = jnp.sin(angle_table)
    new_real = jnp.einsum("gsjd,sa->gajd", real_part, cosine, precision=exact_mode) - jnp.einsum(
        "gsjd,sa->gajd", imag_part, sine_table, precision=exact_mode
    )
    new_imag = jnp.einsum(
        "gsjd,sa->gajd", real_part, sine_table, precision=exact_mode
    ) + jnp.einsum("gsjd,sa->gajd", imag_part, cosine, precision=exact_mode)
    return (new_real, new_imag)


def finish_sections(real_part, imag_part, stride, shards, length):
    sources = jnp.arange(shards, dtype=jnp.int32)
    slower = jnp.arange(stride, dtype=jnp.int32)
    slow_angle = -rotation(slower[:, None], slower[None, :], stride)
    real_part, imag_part = along_slow(real_part, imag_part, slow_angle)
    inner_twist = -rotation(slower[:, None, None], sources[None, None, :], length)
    real_part, imag_part = table_product(
        real_part, imag_part, jnp.cos(inner_twist), jnp.sin(inner_twist)
    )
    last_angle = -rotation(sources[:, None], sources[None, :], shards)
    return along_last(real_part, imag_part, last_angle)


def forward(stacked):
    shards = lax.axis_size("context")
    position = lax.axis_index("context")
    signals, length = stacked.shape
    stride = length // shards
    period = 2 * shards * length
    sources = jnp.arange(shards, dtype=jnp.int32)
    slower = jnp.arange(stride, dtype=jnp.int32)
    blocks = stacked.reshape(signals, stride, shards)
    columns = lax.all_to_all(blocks, "context", split_axis=2, concat_axis=2, tiled=True)
    token_ids = shards * slower[:, None] + position
    order = jnp.arange(2 * shards, dtype=jnp.int32)
    first_angle = -rotation(sources[:, None], order[None, :], 2 * shards)
    real_part = jnp.matmul(columns, jnp.cos(first_angle), precision=exact_mode)
    imag_part = jnp.matmul(columns, jnp.sin(first_angle), precision=exact_mode)
    twist = -rotation(token_ids, order[None, :], period)
    real_part, imag_part = table_product(real_part, imag_part, jnp.cos(twist), jnp.sin(twist))
    spectra = jnp.stack([real_part, imag_part]).reshape(2, signals, stride, 2, shards)
    spectra = lax.all_to_all(spectra, "context", split_axis=4, concat_axis=4, tiled=True)
    real_part, imag_part = finish_sections(spectra[0], spectra[1], stride, shards, length)
    return (real_part, imag_part, order)


def inverse(real_part, imag_part, order):
    shards = lax.axis_size("context")
    position = lax.axis_index("context")
    signals, stride = (real_part.shape[0], real_part.shape[1])
    length = stride * shards
    period = 2 * shards * length
    sources = jnp.arange(shards, dtype=jnp.int32)
    slower = jnp.arange(stride, dtype=jnp.int32)
    last_angle = rotation(sources[:, None], sources[None, :], shards)
    real_part, imag_part = along_last(real_part, imag_part, last_angle)
    inner_twist = rotation(slower[:, None, None], sources[None, None, :], length)
    real_part, imag_part = table_product(
        real_part, imag_part, jnp.cos(inner_twist), jnp.sin(inner_twist)
    )
    slow_angle = rotation(slower[:, None], slower[None, :], stride)
    real_part, imag_part = along_slow(real_part, imag_part, slow_angle)
    spectra = lax.all_to_all(
        jnp.stack([real_part, imag_part]), "context", split_axis=4, concat_axis=4, tiled=True
    )
    real_part = spectra[0].reshape(signals, stride, 2 * shards)
    imag_part = spectra[1].reshape(signals, stride, 2 * shards)
    token_ids = shards * slower[:, None] + position
    twist = rotation(token_ids, order[None, :], period)
    real_part, imag_part = table_product(real_part, imag_part, jnp.cos(twist), jnp.sin(twist))
    first_angle = rotation(order[:, None], sources[None, :], 2 * shards)
    cosine = jnp.cos(first_angle)
    sine_table = jnp.sin(first_angle)
    out_real = jnp.matmul(real_part, cosine, precision=exact_mode) - jnp.matmul(
        imag_part, sine_table, precision=exact_mode
    )
    out_imag = jnp.matmul(real_part, sine_table, precision=exact_mode) + jnp.matmul(
        imag_part, cosine, precision=exact_mode
    )
    results = jnp.stack([out_real, out_imag])
    blocks = lax.all_to_all(results, "context", split_axis=3, concat_axis=3, tiled=True)
    return blocks.reshape(blocks.shape[0], signals, length)


def transform_body(signal, filter_taps, skip_gain, cotangent):
    shards = lax.axis_size("context")
    channels, length = signal.shape
    factor = 1.0 / (2 * shards * length * math.sqrt(shards * length))
    stacked = jnp.concatenate([signal, cotangent, filter_taps[None, :]], axis=0)
    real_part, imag_part, order = forward(stacked)
    sig_re = real_part[:channels]
    sig_im = imag_part[:channels]
    cot_re = real_part[channels : 2 * channels]
    cot_im = imag_part[channels : 2 * channels]
    fil_re = real_part[2 * channels :]
    fil_im = imag_part[2 * channels :]
    out_re = sig_re * fil_re - sig_im * fil_im
    out_im = sig_re * fil_im + sig_im * fil_re
    back_re = cot_re * fil_re + cot_im * fil_im
    back_im = cot_im * fil_re - cot_re * fil_im
    grad_re = jnp.sum(cot_re * sig_re + cot_im * sig_im, axis=0, keepdims=True)
    grad_im = jnp.sum(cot_im * sig_re - cot_re * sig_im, axis=0, keepdims=True)
    restored = inverse(
        jnp.concatenate([out_re - back_im, grad_re], axis=0),
        jnp.concatenate([out_im + back_re, grad_im], axis=0),
        order,
    )
    conv_out = restored[0, :channels]
    conv_back = restored[1, :channels]
    partial_value = restored[0, channels]
    output = conv_out * factor + skip_gain[:, None] * signal
    grad_signal = conv_back * factor + skip_gain[:, None] * cotangent
    grad_filter = lax.psum(partial_value * factor, "chan")
    return (output, grad_signal, grad_filter)


def fits_direct(channels, tokens, shards):
    held = 4 * shards * tokens * (2 * channels + 1)
    scratch = 16 * shards * tokens * channels + 4 * (shards * tokens + LANES) * LANES
    groups = lax.axis_size("chan")
    whole = groups & (groups - 1) == 0 and channels % PACKED_ROWS == 0 and tokens % (8 * LANES) == 0 and shards & (shards - 1) == 0
    return whole and shards > 1 and 2 * held + scratch < KERNEL_BYTES // 2


def body(signal, filter_taps, skip_gain, cotangent):
    channels, tokens = signal.shape
    if fits_direct(channels, tokens, lax.axis_size("context")):
        return direct_body(signal, filter_taps, skip_gain, cotangent)
    return transform_body(signal, filter_taps, skip_gain, cotangent)


def solution(mesh):
    return jax.shard_map(
        body,
        mesh=mesh,
        in_specs=(P("chan", "context"), P("context"), P("chan"), P("chan", "context")),
        out_specs=(P("chan", "context"), P("chan", "context"), P("context")),
        check_vma=False,
    )
```

```python
import functools
import math

import jax
import jax.numpy as jnp
from jax import lax
from jax.experimental import pallas as pl
from jax.experimental.pallas import tpu as pltpu
from jax.sharding import PartitionSpec as P

exact_mode = lax.Precision.HIGHEST

LANES = 128
BLOCK = 256
PACKED_ROWS = 16
KERNEL_BYTES = 16 * 1024 * 1024


def halves(value):
    high = value.astype(jnp.bfloat16)
    low = (value - high.astype(jnp.float32)).astype(jnp.bfloat16)
    return high, low


def dot(left, right, left_dim, right_dim):
    return lax.dot_general(
        left, right, (((left_dim,), (right_dim,)), ((), ())), preferred_element_type=jnp.float32
    )


def dot_halves(left, right, left_dim, right_dim):
    return (
        dot(left[0], right[0], left_dim, right_dim)
        + dot(left[0], right[1], left_dim, right_dim)
        + dot(left[1], right[0], left_dim, right_dim)
    )


def stack_kernel(signal_ref, cotangent_ref, taps_ref, out_ref):
    channels, tokens = signal_ref.shape
    row = 0
    for source in (signal_ref, cotangent_ref):
        for tile in range(tokens // LANES):
            out_ref[row : row + channels, :] = source[:, tile * LANES : (tile + 1) * LANES]
            row += channels
    out_ref[row:, :] = taps_ref[...]


def stack_local(signal, cotangent, taps):
    channels, tokens = signal.shape
    rows = (2 * channels * tokens + tokens) // LANES
    return pl.pallas_call(
        stack_kernel,
        out_shape=pltpu.VMEM((rows, LANES), jnp.float32),
        in_specs=[pl.BlockSpec(memory_space=pltpu.VMEM)] * 3,
        out_specs=pl.BlockSpec(memory_space=pltpu.VMEM),
        name="stack_local",
    )(signal, cotangent, taps.reshape(tokens // LANES, LANES))


def gather_blocks(stacked, shards):
    def flipped(value, bits):
        return lax.ppermute(value, "context", [(i, i ^ bits) for i in range(shards)])

    found = {0: stacked}
    for bits in range(2, shards, 2):
        found[bits] = flipped(stacked, bits)
    for bits in range(0, shards, 2):
        found[bits + 1] = flipped(found[bits], 1)
    return [found[bits] for bits in range(shards)]


def place_rows(block_ref, first, index, channels, tokens, ref, start):
    tiles = tokens // LANES
    for tile in range(tiles):
        rows = first + tile * channels
        both = jnp.concatenate(halves(block_ref[rows : rows + channels, :]), axis=0)
        at = pl.multiple_of((index * tiles + tile) * 2 * channels + start, PACKED_ROWS)
        ref[pl.ds(at, 2 * channels), :] = both


def paired_tiles(ref, start, count, channels, half):
    def rows(tile):
        at = pl.multiple_of((start + tile) * 2 * channels + half * channels, PACKED_ROWS)
        return ref[pl.ds(at, channels), :]

    return jnp.concatenate(
        [jnp.concatenate([rows(tile), rows(tile + 1)], axis=1) for tile in range(0, count, 2)], axis=0
    )


def filter_grad_kernel(shards, channels, tokens, *refs):
    blocks, out_ref, sig, cot, folded = refs[:shards], *refs[shards:]
    me = lax.axis_index("context")
    per, tiles = tokens // BLOCK, tokens // LANES
    count = 2 * tiles * channels
    rows = shards * count
    sig[:count, :] = jnp.zeros((count, LANES), jnp.bfloat16)
    cot[rows:, :] = jnp.zeros((rows, LANES), jnp.bfloat16)
    for bits in range(shards):
        place_rows(blocks[bits], 0, me ^ bits, channels, tokens, sig, count)
        place_rows(blocks[bits], channels * tiles, me ^ bits, channels, tokens, cot, 0)
    held = [paired_tiles(sig, tiles, shards * tiles, channels, half) for half in range(2)]
    for lag in range(per + 1):
        window = [
            paired_tiles(cot, me * tiles + 2 * lag, shards * tiles, channels, half) for half in range(2)
        ]
        folded[:, lag * BLOCK : (lag + 1) * BLOCK] = dot(jnp.concatenate([held[0], held[0], held[1]], axis=0), jnp.concatenate([window[0], window[1], window[0]], axis=0), 0, 0)
    width = (per + 1) * BLOCK - LANES
    total = None
    for group in range(LANES // 8):
        part = (
            folded[8 * group : 8 * group + 8, :width]
            + folded[LANES + 8 * group : LANES + 8 * group + 8, LANES:]
        )
        if group:
            part = pltpu.roll(part, width - 8 * group, 1)
        total = part if total is None else total + part
    row = lax.broadcasted_iota(jnp.int32, total.shape, 0)
    for step in (1, 2, 4):
        total = jnp.where((row & step) != 0, pltpu.roll(total, width - step, 1), total)
    out_ref[...] = jnp.sum(total, axis=0, keepdims=True)[:, :tokens]


def filter_grad(blocks, shards, channels, tokens):
    per = tokens // BLOCK
    rows = shards * per * channels
    return pl.pallas_call(
        functools.partial(filter_grad_kernel, shards, channels, tokens),
        out_shape=[
            jax.ShapeDtypeStruct((1, tokens), jnp.float32),
            pltpu.VMEM((4 * rows // shards * (shards + 1), LANES), jnp.bfloat16),
            pltpu.VMEM((8 * rows, LANES), jnp.bfloat16),
        ],
        in_specs=[pl.BlockSpec(memory_space=pltpu.VMEM)] * shards,
        out_specs=[pl.BlockSpec(memory_space=pltpu.VMEM)] * 3,
        scratch_shapes=[pltpu.VMEM((BLOCK, (per + 1) * BLOCK), jnp.float32)],
        compiler_params=pltpu.CompilerParams(vmem_limit_bytes=KERNEL_BYTES),
        cost_estimate=pl.CostEstimate(
            flops=2 * 3 * (per + 1) * rows * BLOCK * BLOCK, bytes_accessed=4 * rows * BLOCK * 2, transcendentals=0
        ),
        name="filter_grad",
    )(*blocks)


def toeplitz_kernel(shards, channels, tokens, *refs):
    blocks, high_ref, low_ref, taps, skew = refs[:shards], *refs[shards:]
    me = lax.axis_index("context")
    tiles = tokens // LANES
    first = 2 * channels * tiles
    taps[0] = jnp.zeros((tiles, LANES), jnp.float32)
    for bits in range(shards):
        taps[(me ^ bits) + 1] = blocks[bits][first : first + tiles, :]
    high_ref[0] = jnp.zeros((LANES, LANES), jnp.bfloat16)
    low_ref[0] = jnp.zeros((LANES, LANES), jnp.bfloat16)
    width = (tiles + 1) * LANES

    for step in range(shards):
        last, sheet = taps[step], taps[step + 1]
        lines = [last[tiles - 1 : tiles, :]] + [sheet[n : n + 1, :] for n in range(tiles)]
        lean = jnp.concatenate([jnp.broadcast_to(line, (8, LANES)) for line in lines], axis=1)
        lean = pltpu.roll(lean, 0, 1, stride=1, stride_axis=0)
        skew[step] = lean

    def build(step, carry):
        skewed = skew[step]
        for group in range(LANES // PACKED_ROWS):
            top, bottom = (
                pltpu.roll(skewed, PACKED_ROWS * group + rows, 1) if group + rows else skewed
                for rows in (0, 8)
            )
            pair = halves(jnp.concatenate([top, bottom], axis=0))
            for ref, part in zip((high_ref, low_ref), pair):
                for tile in range(tiles):
                    ref[
                        step * tiles + tile + 1, group * PACKED_ROWS : (group + 1) * PACKED_ROWS, :
                    ] = part[:, (tile + 1) * LANES : (tile + 2) * LANES]
        return carry

    lax.fori_loop(0, shards, build, 0, unroll=min(4, shards))


def toeplitz_tiles(blocks, shards, channels, tokens):
    tiles = tokens // LANES
    shape = (shards * tiles + 1, LANES, LANES)
    return pl.pallas_call(
        functools.partial(toeplitz_kernel, shards, channels, tokens),
        out_shape=[pltpu.VMEM(shape, jnp.bfloat16)] * 2,
        in_specs=[pl.BlockSpec(memory_space=pltpu.VMEM)] * shards,
        out_specs=[pl.BlockSpec(memory_space=pltpu.VMEM)] * 2,
        scratch_shapes=[pltpu.VMEM((shards + 1, tiles, LANES), jnp.float32), pltpu.VMEM((shards, 8, (tiles + 1) * LANES), jnp.float32)],
        compiler_params=pltpu.CompilerParams(vmem_limit_bytes=KERNEL_BYTES),
        cost_estimate=pl.CostEstimate(
            flops=16 * shape[0] * LANES * LANES, bytes_accessed=4 * shape[0] * LANES * LANES, transcendentals=0
        ),
        name="toeplitz_tiles",
    )(*blocks)


def convolve_kernel(shards, channels, tokens, *refs):
    own_ref, sig, cot, toe_high, toe_low, gain_ref, out_ref, back_ref, conv, back = refs
    me = lax.axis_index("context")
    tiles = tokens // LANES
    count = 2 * tiles * channels

    def window(ref, tile):
        return ref[pl.ds(pl.multiple_of(tile * 2 * channels, PACKED_ROWS), count), :]

    def forward(lags):
        left = jnp.concatenate([window(sig, (me + 1) * tiles - lag) for lag in lags], axis=1)
        pairs = [jnp.concatenate([toe_high[lag + 1], toe_low[lag + 1]], axis=1) for lag in lags]
        return dot(left, jnp.concatenate(pairs, axis=0), 1, 0)

    def backward(lags):
        left = jnp.concatenate([window(cot, me * tiles + lag) for lag in lags], axis=1)
        pairs = [jnp.concatenate([toe_high[lag + 1], toe_low[lag + 1]], axis=0) for lag in lags]
        return dot(left, jnp.concatenate(pairs, axis=1), 1, 1)

    def total(product, blocks):
        parts = [product([block * tiles + n for n in range(tiles)]) for block in range(blocks)]
        return sum(parts[1:], parts[0])

    def run(index):
        conv[...] = total(forward, index + 1)
        back[...] = total(backward, shards - index)

    for index in range(shards):
        pl.when(me == index)(functools.partial(run, index))
    factor = 1.0 / math.sqrt(shards * tokens)
    square_row = lax.broadcasted_iota(jnp.int32, (channels, channels), 0)
    square_lane = lax.broadcasted_iota(jnp.int32, (channels, channels), 1)
    gain = jnp.sum(
        jnp.where(square_row == square_lane, jnp.broadcast_to(gain_ref[...], (channels, channels)), 0.0),
        axis=1,
        keepdims=True,
    )
    for tile in range(tiles):
        lanes = slice(tile * LANES, (tile + 1) * LANES)
        for ref, value, first in ((out_ref, conv, 0), (back_ref, back, tiles)):
            own = own_ref[(first + tile) * channels : (first + tile + 1) * channels, :]
            top = tile * 2 * channels
            both = value[top : top + channels, :] + value[top + channels : top + 2 * channels, :]
            ref[:, lanes] = (both[:, :LANES] + both[:, LANES:]) * factor + gain * own


def convolve(own, held, toeplitz, skip_gain, shards, channels, tokens):
    count = 2 * channels * tokens // LANES
    return pl.pallas_call(
        functools.partial(convolve_kernel, shards, channels, tokens),
        out_shape=[jax.ShapeDtypeStruct((channels, tokens), jnp.float32)] * 2,
        in_specs=[pl.BlockSpec(memory_space=pltpu.VMEM)] * 6,
        out_specs=[pl.BlockSpec(memory_space=pltpu.VMEM)] * 2,
        scratch_shapes=[pltpu.VMEM((count, 2 * LANES), jnp.float32)] * 2,
        compiler_params=pltpu.CompilerParams(vmem_limit_bytes=KERNEL_BYTES),
        cost_estimate=pl.CostEstimate(
            flops=2 * (shards + 1) * tokens * count * 2 * LANES,
            bytes_accessed=8 * shards * count * LANES,
            transcendentals=0,
        ),
        name="convolve",
    )(own, *held, *toeplitz, skip_gain.reshape(1, channels))


def direct_body(signal, filter_taps, skip_gain, cotangent):
    shards, groups = lax.axis_size("context"), lax.axis_size("chan")
    channels, tokens = signal.shape
    stacked = stack_local(signal, cotangent, filter_taps)
    blocks = gather_blocks(stacked, shards)
    value, *held = filter_grad(blocks, shards, channels, tokens)
    toeplitz = toeplitz_tiles(blocks, shards, channels, tokens)
    bits = 1
    while bits < groups:
        value = value + lax.ppermute(value, "chan", [(i, i ^ bits) for i in range(groups)])
        if bits == 1:
            value, *toeplitz = lax.optimization_barrier((value, *toeplitz))
        bits *= 2
    output, grad_signal = convolve(blocks[0], held, toeplitz, skip_gain, shards, channels, tokens)
    grad_filter = value.reshape(tokens) * (1.0 / math.sqrt(shards * tokens))
    return (output, grad_signal, grad_filter)


def rotation(first, second, period):
    turned = first * second % period
    return turned.astype(jnp.float32) * (2.0 * math.pi / period)


def table_product(real_part, imag_part, cosine, sine_table):
    return (
        real_part * cosine - imag_part * sine_table,
        real_part * sine_table + imag_part * cosine,
    )


def along_last(real_part, imag_part, angle_table):
    cosine = jnp.cos(angle_table)
    sine_table = jnp.sin(angle_table)
    new_real = jnp.matmul(real_part, cosine, precision=exact_mode) - jnp.matmul(
        imag_part, sine_table, precision=exact_mode
    )
    new_imag = jnp.matmul(real_part, sine_table, precision=exact_mode) + jnp.matmul(
        imag_part, cosine, precision=exact_mode
    )
    return (new_real, new_imag)


def along_slow(real_part, imag_part, angle_table):
    cosine = jnp.cos(angle_table)
    sine_table = jnp.sin(angle_table)
    new_real = jnp.einsum("gsjd,sa->gajd", real_part, cosine, precision=exact_mode) - jnp.einsum(
        "gsjd,sa->gajd", imag_part, sine_table, precision=exact_mode
    )
    new_imag = jnp.einsum(
        "gsjd,sa->gajd", real_part, sine_table, precision=exact_mode
    ) + jnp.einsum("gsjd,sa->gajd", imag_part, cosine, precision=exact_mode)
    return (new_real, new_imag)


def finish_sections(real_part, imag_part, stride, shards, length):
    sources = jnp.arange(shards, dtype=jnp.int32)
    slower = jnp.arange(stride, dtype=jnp.int32)
    slow_angle = -rotation(slower[:, None], slower[None, :], stride)
    real_part, imag_part = along_slow(real_part, imag_part, slow_angle)
    inner_twist = -rotation(slower[:, None, None], sources[None, None, :], length)
    real_part, imag_part = table_product(
        real_part, imag_part, jnp.cos(inner_twist), jnp.sin(inner_twist)
    )
    last_angle = -rotation(sources[:, None], sources[None, :], shards)
    return along_last(real_part, imag_part, last_angle)


def forward(stacked):
    shards = lax.axis_size("context")
    position = lax.axis_index("context")
    signals, length = stacked.shape
    stride = length // shards
    period = 2 * shards * length
    sources = jnp.arange(shards, dtype=jnp.int32)
    slower = jnp.arange(stride, dtype=jnp.int32)
    blocks = stacked.reshape(signals, stride, shards)
    columns = lax.all_to_all(blocks, "context", split_axis=2, concat_axis=2, tiled=True)
    token_ids = shards * slower[:, None] + position
    order = jnp.arange(2 * shards, dtype=jnp.int32)
    first_angle = -rotation(sources[:, None], order[None, :], 2 * shards)
    real_part = jnp.matmul(columns, jnp.cos(first_angle), precision=exact_mode)
    imag_part = jnp.matmul(columns, jnp.sin(first_angle), precision=exact_mode)
    twist = -rotation(token_ids, order[None, :], period)
    real_part, imag_part = table_product(real_part, imag_part, jnp.cos(twist), jnp.sin(twist))
    spectra = jnp.stack([real_part, imag_part]).reshape(2, signals, stride, 2, shards)
    spectra = lax.all_to_all(spectra, "context", split_axis=4, concat_axis=4, tiled=True)
    real_part, imag_part = finish_sections(spectra[0], spectra[1], stride, shards, length)
    return (real_part, imag_part, order)


def inverse(real_part, imag_part, order):
    shards = lax.axis_size("context")
    position = lax.axis_index("context")
    signals, stride = (real_part.shape[0], real_part.shape[1])
    length = stride * shards
    period = 2 * shards * length
    sources = jnp.arange(shards, dtype=jnp.int32)
    slower = jnp.arange(stride, dtype=jnp.int32)
    last_angle = rotation(sources[:, None], sources[None, :], shards)
    real_part, imag_part = along_last(real_part, imag_part, last_angle)
    inner_twist = rotation(slower[:, None, None], sources[None, None, :], length)
    real_part, imag_part = table_product(
        real_part, imag_part, jnp.cos(inner_twist), jnp.sin(inner_twist)
    )
    slow_angle = rotation(slower[:, None], slower[None, :], stride)
    real_part, imag_part = along_slow(real_part, imag_part, slow_angle)
    spectra = lax.all_to_all(
        jnp.stack([real_part, imag_part]), "context", split_axis=4, concat_axis=4, tiled=True
    )
    real_part = spectra[0].reshape(signals, stride, 2 * shards)
    imag_part = spectra[1].reshape(signals, stride, 2 * shards)
    token_ids = shards * slower[:, None] + position
    twist = rotation(token_ids, order[None, :], period)
    real_part, imag_part = table_product(real_part, imag_part, jnp.cos(twist), jnp.sin(twist))
    first_angle = rotation(order[:, None], sources[None, :], 2 * shards)
    cosine = jnp.cos(first_angle)
    sine_table = jnp.sin(first_angle)
    out_real = jnp.matmul(real_part, cosine, precision=exact_mode) - jnp.matmul(
        imag_part, sine_table, precision=exact_mode
    )
    out_imag = jnp.matmul(real_part, sine_table, precision=exact_mode) + jnp.matmul(
        imag_part, cosine, precision=exact_mode
    )
    results = jnp.stack([out_real, out_imag])
    blocks = lax.all_to_all(results, "context", split_axis=3, concat_axis=3, tiled=True)
    return blocks.reshape(blocks.shape[0], signals, length)


def transform_body(signal, filter_taps, skip_gain, cotangent):
    shards = lax.axis_size("context")
    channels, length = signal.shape
    factor = 1.0 / (2 * shards * length * math.sqrt(shards * length))
    stacked = jnp.concatenate([signal, cotangent, filter_taps[None, :]], axis=0)
    real_part, imag_part, order = forward(stacked)
    sig_re = real_part[:channels]
    sig_im = imag_part[:channels]
    cot_re = real_part[channels : 2 * channels]
    cot_im = imag_part[channels : 2 * channels]
    fil_re = real_part[2 * channels :]
    fil_im = imag_part[2 * channels :]
    out_re = sig_re * fil_re - sig_im * fil_im
    out_im = sig_re * fil_im + sig_im * fil_re
    back_re = cot_re * fil_re + cot_im * fil_im
    back_im = cot_im * fil_re - cot_re * fil_im
    grad_re = jnp.sum(cot_re * sig_re + cot_im * sig_im, axis=0, keepdims=True)
    grad_im = jnp.sum(cot_im * sig_re - cot_re * sig_im, axis=0, keepdims=True)
    restored = inverse(
        jnp.concatenate([out_re - back_im, grad_re], axis=0),
        jnp.concatenate([out_im + back_re, grad_im], axis=0),
        order,
    )
    conv_out = restored[0, :channels]
    conv_back = restored[1, :channels]
    partial_value = restored[0, channels]
    output = conv_out * factor + skip_gain[:, None] * signal
    grad_signal = conv_back * factor + skip_gain[:, None] * cotangent
    grad_filter = lax.psum(partial_value * factor, "chan")
    return (output, grad_signal, grad_filter)


def fits_direct(channels, tokens, shards):
    held = 4 * shards * tokens * (2 * channels + 1)
    scratch = 16 * shards * tokens * channels + 4 * (shards * tokens + LANES) * LANES
    groups = lax.axis_size("chan")
    whole = groups & (groups - 1) == 0 and channels % PACKED_ROWS == 0 and tokens % (8 * LANES) == 0 and shards & (shards - 1) == 0
    return whole and shards > 1 and 2 * held + scratch < KERNEL_BYTES


def body(signal, filter_taps, skip_gain, cotangent):
    channels, tokens = signal.shape
    if fits_direct(channels, tokens, lax.axis_size("context")):
        return direct_body(signal, filter_taps, skip_gain, cotangent)
    return transform_body(signal, filter_taps, skip_gain, cotangent)


def solution(mesh):
    return jax.shard_map(
        body,
        mesh=mesh,
        in_specs=(P("chan", "context"), P("context"), P("chan"), P("chan", "context")),
        out_specs=(P("chan", "context"), P("chan", "context"), P("context")),
        check_vma=False,
    )
```

```python
import functools
import math

import jax
import jax.numpy as jnp
from jax import lax
from jax.experimental import pallas as pl
from jax.experimental.pallas import tpu as pltpu
from jax.sharding import PartitionSpec as P

exact_mode = lax.Precision.HIGHEST

LANES = 128
BLOCK = 256
PACKED_ROWS = 16
EARLY = 2
KERNEL_BYTES = 16 * 1024 * 1024


def halves(value):
    high = value.astype(jnp.bfloat16)
    low = (value - high.astype(jnp.float32)).astype(jnp.bfloat16)
    return high, low


def dot(left, right, left_dim, right_dim):
    return lax.dot_general(
        left, right, (((left_dim,), (right_dim,)), ((), ())), preferred_element_type=jnp.float32
    )


def dot_halves(left, right, left_dim, right_dim):
    return (
        dot(left[0], right[0], left_dim, right_dim)
        + dot(left[0], right[1], left_dim, right_dim)
        + dot(left[1], right[0], left_dim, right_dim)
    )


def stack_kernel(signal_ref, cotangent_ref, taps_ref, out_ref):
    channels, tokens = signal_ref.shape
    row = 0
    for source in (signal_ref, cotangent_ref):
        for tile in range(tokens // LANES):
            out_ref[row : row + channels, :] = source[:, tile * LANES : (tile + 1) * LANES]
            row += channels
    out_ref[row:, :] = taps_ref[...]


def stack_local(signal, cotangent, taps):
    channels, tokens = signal.shape
    rows = (2 * channels * tokens + tokens) // LANES
    return pl.pallas_call(
        stack_kernel,
        out_shape=pltpu.VMEM((rows, LANES), jnp.float32),
        in_specs=[pl.BlockSpec(memory_space=pltpu.VMEM)] * 3,
        out_specs=pl.BlockSpec(memory_space=pltpu.VMEM),
        name="stack_local",
    )(signal, cotangent, taps.reshape(tokens // LANES, LANES))


def gather_blocks(stacked, shards):
    def flipped(value, bits):
        return lax.ppermute(value, "context", [(i, i ^ bits) for i in range(shards)])

    found = {0: stacked}
    for bits in range(2, shards, 2):
        found[bits] = flipped(stacked, bits)
    for bits in range(0, shards, 2):
        found[bits + 1] = flipped(found[bits], 1)
    return [found[bits] for bits in range(shards)]


def place_rows(block_ref, first, index, channels, tokens, ref, start):
    tiles = tokens // LANES
    for tile in range(tiles):
        rows = first + tile * channels
        both = jnp.concatenate(halves(block_ref[rows : rows + channels, :]), axis=0)
        at = pl.multiple_of((index * tiles + tile) * 2 * channels + start, PACKED_ROWS)
        ref[pl.ds(at, 2 * channels), :] = both


def paired_tiles(ref, start, count, channels, half):
    def rows(tile):
        at = pl.multiple_of((start + tile) * 2 * channels + half * channels, PACKED_ROWS)
        return ref[pl.ds(at, channels), :]

    return jnp.concatenate(
        [jnp.concatenate([rows(tile), rows(tile + 1)], axis=1) for tile in range(0, count, 2)], axis=0
    )


def filter_grad_kernel(shards, channels, tokens, *refs):
    blocks, out_ref, sig, cot, folded = refs[:shards], *refs[shards:]
    me = lax.axis_index("context")
    per, tiles = tokens // BLOCK, tokens // LANES
    count = 2 * tiles * channels
    rows = shards * count
    sig[:count, :] = jnp.zeros((count, LANES), jnp.bfloat16)
    cot[rows:, :] = jnp.zeros((rows, LANES), jnp.bfloat16)
    for bits in range(shards):
        place_rows(blocks[bits], 0, me ^ bits, channels, tokens, sig, count)
        place_rows(blocks[bits], channels * tiles, me ^ bits, channels, tokens, cot, 0)
    held = [paired_tiles(sig, tiles, shards * tiles, channels, half) for half in range(2)]
    for lag in range(per + 1):
        window = [
            paired_tiles(cot, me * tiles + 2 * lag, shards * tiles, channels, half) for half in range(2)
        ]
        folded[:, lag * BLOCK : (lag + 1) * BLOCK] = dot(jnp.concatenate([held[0], held[0], held[1]], axis=0), jnp.concatenate([window[0], window[1], window[0]], axis=0), 0, 0)
    width = (per + 1) * BLOCK - LANES
    total = None
    for group in range(LANES // 8):
        part = (
            folded[8 * group : 8 * group + 8, :width]
            + folded[LANES + 8 * group : LANES + 8 * group + 8, LANES:]
        )
        if group:
            part = pltpu.roll(part, width - 8 * group, 1)
        total = part if total is None else total + part
    row = lax.broadcasted_iota(jnp.int32, total.shape, 0)
    for step in (1, 2, 4):
        total = jnp.where((row & step) != 0, pltpu.roll(total, width - step, 1), total)
    out_ref[...] = jnp.sum(total, axis=0, keepdims=True)[:, :tokens]


def filter_grad(blocks, shards, channels, tokens):
    per = tokens // BLOCK
    rows = shards * per * channels
    return pl.pallas_call(
        functools.partial(filter_grad_kernel, shards, channels, tokens),
        out_shape=[
            jax.ShapeDtypeStruct((1, tokens), jnp.float32),
            pltpu.VMEM((4 * rows // shards * (shards + 1), LANES), jnp.bfloat16),
            pltpu.VMEM((8 * rows, LANES), jnp.bfloat16),
        ],
        in_specs=[pl.BlockSpec(memory_space=pltpu.VMEM)] * shards,
        out_specs=[pl.BlockSpec(memory_space=pltpu.VMEM)] * 3,
        scratch_shapes=[pltpu.VMEM((BLOCK, (per + 1) * BLOCK), jnp.float32)],
        compiler_params=pltpu.CompilerParams(vmem_limit_bytes=KERNEL_BYTES),
        cost_estimate=pl.CostEstimate(
            flops=2 * 3 * (per + 1) * rows * BLOCK * BLOCK, bytes_accessed=4 * rows * BLOCK * 2, transcendentals=0
        ),
        name="filter_grad",
    )(*blocks)


def convolve_block(held, me, tiles, channels, toe_high, toe_low, block, adjoint):
    count = 2 * tiles * channels
    lags = [block * tiles + n for n in range(tiles)]

    def window(lag):
        tile = me * tiles + lag if adjoint else (me + 1) * tiles - lag
        return held[pl.ds(pl.multiple_of(tile * 2 * channels, PACKED_ROWS), count), :]

    side = 0 if adjoint else 1
    left = jnp.concatenate([window(lag) for lag in lags], axis=1)
    pairs = [jnp.concatenate([toe_high[lag + 1], toe_low[lag + 1]], axis=side) for lag in lags]
    return dot(left, jnp.concatenate(pairs, axis=1 - side), 1, 1 - side)


def toeplitz_kernel(shards, channels, tokens, early, *refs):
    blocks, sig, cot, high_ref, low_ref, start_ref, taps, skew = refs[:shards], *refs[shards:]
    me = lax.axis_index("context")
    tiles = tokens // LANES
    first = 2 * channels * tiles
    taps[0] = jnp.zeros((tiles, LANES), jnp.float32)
    for bits in range(shards):
        taps[(me ^ bits) + 1] = blocks[bits][first : first + tiles, :]
    high_ref[0] = jnp.zeros((LANES, LANES), jnp.bfloat16)
    low_ref[0] = jnp.zeros((LANES, LANES), jnp.bfloat16)
    width = (tiles + 1) * LANES

    for step in range(shards):
        last, sheet = taps[step], taps[step + 1]
        lines = [last[tiles - 1 : tiles, :]] + [sheet[n : n + 1, :] for n in range(tiles)]
        lean = jnp.concatenate([jnp.broadcast_to(line, (8, LANES)) for line in lines], axis=1)
        lean = pltpu.roll(lean, 0, 1, stride=1, stride_axis=0)
        skew[step] = lean

    def build(step, carry):
        skewed = skew[step]
        for group in range(LANES // PACKED_ROWS):
            top, bottom = (
                pltpu.roll(skewed, PACKED_ROWS * group + rows, 1) if group + rows else skewed
                for rows in (0, 8)
            )
            pair = halves(jnp.concatenate([top, bottom], axis=0))
            for ref, part in zip((high_ref, low_ref), pair):
                for tile in range(tiles):
                    ref[
                        step * tiles + tile + 1, group * PACKED_ROWS : (group + 1) * PACKED_ROWS, :
                    ] = part[:, (tile + 1) * LANES : (tile + 2) * LANES]
        return carry

    lax.fori_loop(0, shards, build, 0, unroll=min(4, shards))

    def begin(held, adjoint):
        parts = [
            convolve_block(held, me, tiles, channels, high_ref, low_ref, block, adjoint) for block in range(early)
        ]
        start_ref[...] = sum(parts[1:], parts[0])

    pl.when(me >= shards // 2)(functools.partial(begin, sig, False))
    pl.when(me < shards // 2)(functools.partial(begin, cot, True))


def toeplitz_tiles(blocks, held, shards, channels, tokens, early):
    tiles = tokens // LANES
    shape = (shards * tiles + 1, LANES, LANES)
    return pl.pallas_call(
        functools.partial(toeplitz_kernel, shards, channels, tokens, early),
        out_shape=[pltpu.VMEM(shape, jnp.bfloat16)] * 2
        + [pltpu.VMEM((2 * channels * tiles, 2 * LANES), jnp.float32)],
        in_specs=[pl.BlockSpec(memory_space=pltpu.VMEM)] * (shards + 2),
        out_specs=[pl.BlockSpec(memory_space=pltpu.VMEM)] * 3,
        scratch_shapes=[pltpu.VMEM((shards + 1, tiles, LANES), jnp.float32), pltpu.VMEM((shards, 8, (tiles + 1) * LANES), jnp.float32)],
        compiler_params=pltpu.CompilerParams(vmem_limit_bytes=KERNEL_BYTES),
        cost_estimate=pl.CostEstimate(
            flops=16 * shape[0] * LANES * LANES, bytes_accessed=4 * shape[0] * LANES * LANES, transcendentals=0
        ),
        name="toeplitz_tiles",
    )(*blocks, *held)


def convolve_kernel(shards, channels, tokens, early, *refs):
    own_ref, sig, cot, toe_high, toe_low, start_ref, gain_ref, out_ref, back_ref, conv, back = refs
    me = lax.axis_index("context")
    tiles = tokens // LANES

    def total(held, blocks, adjoint, begun):
        parts = [start_ref[...]] if begun else []
        for block in range(early if begun else 0, blocks):
            parts.append(convolve_block(held, me, tiles, channels, toe_high, toe_low, block, adjoint))
        return sum(parts[1:], parts[0])

    def run(index):
        conv[...] = total(sig, index + 1, False, index >= shards // 2)
        back[...] = total(cot, shards - index, True, index < shards // 2)

    for index in range(shards):
        pl.when(me == index)(functools.partial(run, index))
    factor = 1.0 / math.sqrt(shards * tokens)
    square_row = lax.broadcasted_iota(jnp.int32, (channels, channels), 0)
    square_lane = lax.broadcasted_iota(jnp.int32, (channels, channels), 1)
    gain = jnp.sum(
        jnp.where(square_row == square_lane, jnp.broadcast_to(gain_ref[...], (channels, channels)), 0.0),
        axis=1,
        keepdims=True,
    )
    for tile in range(tiles):
        lanes = slice(tile * LANES, (tile + 1) * LANES)
        for ref, value, first in ((out_ref, conv, 0), (back_ref, back, tiles)):
            own = own_ref[(first + tile) * channels : (first + tile + 1) * channels, :]
            top = tile * 2 * channels
            both = value[top : top + channels, :] + value[top + channels : top + 2 * channels, :]
            ref[:, lanes] = (both[:, :LANES] + both[:, LANES:]) * factor + gain * own


def convolve(own, held, toeplitz, skip_gain, shards, channels, tokens, early):
    count = 2 * channels * tokens // LANES
    return pl.pallas_call(
        functools.partial(convolve_kernel, shards, channels, tokens, early),
        out_shape=[jax.ShapeDtypeStruct((channels, tokens), jnp.float32)] * 2,
        in_specs=[pl.BlockSpec(memory_space=pltpu.VMEM)] * 7,
        out_specs=[pl.BlockSpec(memory_space=pltpu.VMEM)] * 2,
        scratch_shapes=[pltpu.VMEM((count, 2 * LANES), jnp.float32)] * 2,
        compiler_params=pltpu.CompilerParams(vmem_limit_bytes=KERNEL_BYTES),
        cost_estimate=pl.CostEstimate(
            flops=2 * (shards + 1) * tokens * count * 2 * LANES,
            bytes_accessed=8 * shards * count * LANES,
            transcendentals=0,
        ),
        name="convolve",
    )(own, *held, *toeplitz, skip_gain.reshape(1, channels))


def direct_body(signal, filter_taps, skip_gain, cotangent):
    shards, groups = lax.axis_size("context"), lax.axis_size("chan")
    channels, tokens = signal.shape
    stacked = stack_local(signal, cotangent, filter_taps)
    blocks = gather_blocks(stacked, shards)
    value, *held = filter_grad(blocks, shards, channels, tokens)
    toeplitz = toeplitz_tiles(blocks, held, shards, channels, tokens, EARLY)
    bits = 1
    while bits < groups:
        value = value + lax.ppermute(value, "chan", [(i, i ^ bits) for i in range(groups)])
        if bits == 1:
            value, *toeplitz = lax.optimization_barrier((value, *toeplitz))
        bits *= 2
    output, grad_signal = convolve(blocks[0], held, toeplitz, skip_gain, shards, channels, tokens, EARLY)
    grad_filter = value.reshape(tokens) * (1.0 / math.sqrt(shards * tokens))
    return (output, grad_signal, grad_filter)


def rotation(first, second, period):
    turned = first * second % period
    return turned.astype(jnp.float32) * (2.0 * math.pi / period)


def table_product(real_part, imag_part, cosine, sine_table):
    return (
        real_part * cosine - imag_part * sine_table,
        real_part * sine_table + imag_part * cosine,
    )


def along_last(real_part, imag_part, angle_table):
    cosine = jnp.cos(angle_table)
    sine_table = jnp.sin(angle_table)
    new_real = jnp.matmul(real_part, cosine, precision=exact_mode) - jnp.matmul(
        imag_part, sine_table, precision=exact_mode
    )
    new_imag = jnp.matmul(real_part, sine_table, precision=exact_mode) + jnp.matmul(
        imag_part, cosine, precision=exact_mode
    )
    return (new_real, new_imag)


def along_slow(real_part, imag_part, angle_table):
    cosine = jnp.cos(angle_table)
    sine_table = jnp.sin(angle_table)
    new_real = jnp.einsum("gsjd,sa->gajd", real_part, cosine, precision=exact_mode) - jnp.einsum(
        "gsjd,sa->gajd", imag_part, sine_table, precision=exact_mode
    )
    new_imag = jnp.einsum(
        "gsjd,sa->gajd", real_part, sine_table, precision=exact_mode
    ) + jnp.einsum("gsjd,sa->gajd", imag_part, cosine, precision=exact_mode)
    return (new_real, new_imag)


def finish_sections(real_part, imag_part, stride, shards, length):
    sources = jnp.arange(shards, dtype=jnp.int32)
    slower = jnp.arange(stride, dtype=jnp.int32)
    slow_angle = -rotation(slower[:, None], slower[None, :], stride)
    real_part, imag_part = along_slow(real_part, imag_part, slow_angle)
    inner_twist = -rotation(slower[:, None, None], sources[None, None, :], length)
    real_part, imag_part = table_product(
        real_part, imag_part, jnp.cos(inner_twist), jnp.sin(inner_twist)
    )
    last_angle = -rotation(sources[:, None], sources[None, :], shards)
    return along_last(real_part, imag_part, last_angle)


def forward(stacked):
    shards = lax.axis_size("context")
    position = lax.axis_index("context")
    signals, length = stacked.shape
    stride = length // shards
    period = 2 * shards * length
    sources = jnp.arange(shards, dtype=jnp.int32)
    slower = jnp.arange(stride, dtype=jnp.int32)
    blocks = stacked.reshape(signals, stride, shards)
    columns = lax.all_to_all(blocks, "context", split_axis=2, concat_axis=2, tiled=True)
    token_ids = shards * slower[:, None] + position
    order = jnp.arange(2 * shards, dtype=jnp.int32)
    first_angle = -rotation(sources[:, None], order[None, :], 2 * shards)
    real_part = jnp.matmul(columns, jnp.cos(first_angle), precision=exact_mode)
    imag_part = jnp.matmul(columns, jnp.sin(first_angle), precision=exact_mode)
    twist = -rotation(token_ids, order[None, :], period)
    real_part, imag_part = table_product(real_part, imag_part, jnp.cos(twist), jnp.sin(twist))
    spectra = jnp.stack([real_part, imag_part]).reshape(2, signals, stride, 2, shards)
    spectra = lax.all_to_all(spectra, "context", split_axis=4, concat_axis=4, tiled=True)
    real_part, imag_part = finish_sections(spectra[0], spectra[1], stride, shards, length)
    return (real_part, imag_part, order)


def inverse(real_part, imag_part, order):
    shards = lax.axis_size("context")
    position = lax.axis_index("context")
    signals, stride = (real_part.shape[0], real_part.shape[1])
    length = stride * shards
    period = 2 * shards * length
    sources = jnp.arange(shards, dtype=jnp.int32)
    slower = jnp.arange(stride, dtype=jnp.int32)
    last_angle = rotation(sources[:, None], sources[None, :], shards)
    real_part, imag_part = along_last(real_part, imag_part, last_angle)
    inner_twist = rotation(slower[:, None, None], sources[None, None, :], length)
    real_part, imag_part = table_product(
        real_part, imag_part, jnp.cos(inner_twist), jnp.sin(inner_twist)
    )
    slow_angle = rotation(slower[:, None], slower[None, :], stride)
    real_part, imag_part = along_slow(real_part, imag_part, slow_angle)
    spectra = lax.all_to_all(
        jnp.stack([real_part, imag_part]), "context", split_axis=4, concat_axis=4, tiled=True
    )
    real_part = spectra[0].reshape(signals, stride, 2 * shards)
    imag_part = spectra[1].reshape(signals, stride, 2 * shards)
    token_ids = shards * slower[:, None] + position
    twist = rotation(token_ids, order[None, :], period)
    real_part, imag_part = table_product(real_part, imag_part, jnp.cos(twist), jnp.sin(twist))
    first_angle = rotation(order[:, None], sources[None, :], 2 * shards)
    cosine = jnp.cos(first_angle)
    sine_table = jnp.sin(first_angle)
    out_real = jnp.matmul(real_part, cosine, precision=exact_mode) - jnp.matmul(
        imag_part, sine_table, precision=exact_mode
    )
    out_imag = jnp.matmul(real_part, sine_table, precision=exact_mode) + jnp.matmul(
        imag_part, cosine, precision=exact_mode
    )
    results = jnp.stack([out_real, out_imag])
    blocks = lax.all_to_all(results, "context", split_axis=3, concat_axis=3, tiled=True)
    return blocks.reshape(blocks.shape[0], signals, length)


def transform_body(signal, filter_taps, skip_gain, cotangent):
    shards = lax.axis_size("context")
    channels, length = signal.shape
    factor = 1.0 / (2 * shards * length * math.sqrt(shards * length))
    stacked = jnp.concatenate([signal, cotangent, filter_taps[None, :]], axis=0)
    real_part, imag_part, order = forward(stacked)
    sig_re = real_part[:channels]
    sig_im = imag_part[:channels]
    cot_re = real_part[channels : 2 * channels]
    cot_im = imag_part[channels : 2 * channels]
    fil_re = real_part[2 * channels :]
    fil_im = imag_part[2 * channels :]
    out_re = sig_re * fil_re - sig_im * fil_im
    out_im = sig_re * fil_im + sig_im * fil_re
    back_re = cot_re * fil_re + cot_im * fil_im
    back_im = cot_im * fil_re - cot_re * fil_im
    grad_re = jnp.sum(cot_re * sig_re + cot_im * sig_im, axis=0, keepdims=True)
    grad_im = jnp.sum(cot_im * sig_re - cot_re * sig_im, axis=0, keepdims=True)
    restored = inverse(
        jnp.concatenate([out_re - back_im, grad_re], axis=0),
        jnp.concatenate([out_im + back_re, grad_im], axis=0),
        order,
    )
    conv_out = restored[0, :channels]
    conv_back = restored[1, :channels]
    partial_value = restored[0, channels]
    output = conv_out * factor + skip_gain[:, None] * signal
    grad_signal = conv_back * factor + skip_gain[:, None] * cotangent
    grad_filter = lax.psum(partial_value * factor, "chan")
    return (output, grad_signal, grad_filter)


def fits_direct(channels, tokens, shards):
    held = 4 * shards * tokens * (2 * channels + 1)
    scratch = 16 * shards * tokens * channels + 4 * (shards * tokens + LANES) * LANES
    groups = lax.axis_size("chan")
    whole = groups & (groups - 1) == 0 and channels % PACKED_ROWS == 0 and tokens % (8 * LANES) == 0 and shards & (shards - 1) == 0
    return whole and shards >= 2 * EARLY and 2 * held + scratch < KERNEL_BYTES


def body(signal, filter_taps, skip_gain, cotangent):
    channels, tokens = signal.shape
    if fits_direct(channels, tokens, lax.axis_size("context")):
        return direct_body(signal, filter_taps, skip_gain, cotangent)
    return transform_body(signal, filter_taps, skip_gain, cotangent)


def solution(mesh):
    return jax.shard_map(
        body,
        mesh=mesh,
        in_specs=(P("chan", "context"), P("context"), P("chan"), P("chan", "context")),
        out_specs=(P("chan", "context"), P("chan", "context"), P("context")),
        check_vma=False,
    )
```

```python
import functools
import math

import jax
import jax.numpy as jnp
from jax import lax
from jax.experimental import pallas as pl
from jax.experimental.pallas import tpu as pltpu
from jax.sharding import PartitionSpec as P

exact_mode = lax.Precision.HIGHEST

LANES = 128
BLOCK = 256
PACKED_ROWS = 16
KERNEL_BYTES = 16 * 1024 * 1024


def halves(value):
    high = value.astype(jnp.bfloat16)
    low = (value - high.astype(jnp.float32)).astype(jnp.bfloat16)
    return high, low


def dot(left, right, left_dim, right_dim):
    return lax.dot_general(
        left, right, (((left_dim,), (right_dim,)), ((), ())), preferred_element_type=jnp.float32
    )


def dot_halves(left, right, left_dim, right_dim):
    return (
        dot(left[0], right[0], left_dim, right_dim)
        + dot(left[0], right[1], left_dim, right_dim)
        + dot(left[1], right[0], left_dim, right_dim)
    )


def stack_kernel(signal_ref, cotangent_ref, taps_ref, out_ref):
    channels, tokens = signal_ref.shape
    row = 0
    for source in (signal_ref, cotangent_ref):
        for tile in range(tokens // LANES):
            out_ref[row : row + channels, :] = source[:, tile * LANES : (tile + 1) * LANES]
            row += channels
    out_ref[row:, :] = taps_ref[...]


def stack_local(signal, cotangent, taps):
    channels, tokens = signal.shape
    rows = (2 * channels * tokens + tokens) // LANES
    return pl.pallas_call(
        stack_kernel,
        out_shape=pltpu.VMEM((rows, LANES), jnp.float32),
        in_specs=[pl.BlockSpec(memory_space=pltpu.VMEM)] * 3,
        out_specs=pl.BlockSpec(memory_space=pltpu.VMEM),
        name="stack_local",
    )(signal, cotangent, taps.reshape(tokens // LANES, LANES))


def gather_blocks(stacked, shards):
    def flipped(value, bits):
        return lax.ppermute(value, "context", [(i, i ^ bits) for i in range(shards)])

    found = {0: stacked}
    for bits in range(2, shards, 2):
        found[bits] = flipped(stacked, bits)
    for bits in range(0, shards, 2):
        found[bits + 1] = flipped(found[bits], 1)
    return [found[bits] for bits in range(shards)]


def place_rows(block_ref, first, index, channels, tokens, ref, start):
    tiles = tokens // LANES
    for tile in range(tiles):
        rows = first + tile * channels
        both = jnp.concatenate(halves(block_ref[rows : rows + channels, :]), axis=0)
        at = pl.multiple_of((index * tiles + tile) * 2 * channels + start, PACKED_ROWS)
        ref[pl.ds(at, 2 * channels), :] = both


def paired_tiles(ref, start, count, channels, half):
    def rows(tile):
        at = pl.multiple_of((start + tile) * 2 * channels + half * channels, PACKED_ROWS)
        return ref[pl.ds(at, channels), :]

    return jnp.concatenate(
        [jnp.concatenate([rows(tile), rows(tile + 1)], axis=1) for tile in range(0, count, 2)], axis=0
    )


def filter_grad_kernel(shards, channels, tokens, *refs):
    blocks, out_ref, sig, cot, folded = refs[:shards], *refs[shards:]
    me = lax.axis_index("context")
    per, tiles = tokens // BLOCK, tokens // LANES
    count = 2 * tiles * channels
    rows = shards * count
    sig[:count, :] = jnp.zeros((count, LANES), jnp.bfloat16)
    cot[rows:, :] = jnp.zeros((rows, LANES), jnp.bfloat16)
    for bits in range(shards):
        place_rows(blocks[bits], 0, me ^ bits, channels, tokens, sig, count)
        place_rows(blocks[bits], channels * tiles, me ^ bits, channels, tokens, cot, 0)
    held = [paired_tiles(sig, tiles, shards * tiles, channels, half) for half in range(2)]
    for lag in range(per + 1):
        window = [
            paired_tiles(cot, me * tiles + 2 * lag, shards * tiles, channels, half) for half in range(2)
        ]
        folded[:, lag * BLOCK : (lag + 1) * BLOCK] = dot(jnp.concatenate([held[0], held[0], held[1]], axis=0), jnp.concatenate([window[0], window[1], window[0]], axis=0), 0, 0)
    width = (per + 1) * BLOCK - LANES
    total = None
    for group in range(LANES // 8):
        part = (
            folded[8 * group : 8 * group + 8, :width]
            + folded[LANES + 8 * group : LANES + 8 * group + 8, LANES:]
        )
        if group:
            part = pltpu.roll(part, width - 8 * group, 1)
        total = part if total is None else total + part
    row = lax.broadcasted_iota(jnp.int32, total.shape, 0)
    for step in (1, 2, 4):
        total = jnp.where((row & step) != 0, pltpu.roll(total, width - step, 1), total)
    out_ref[...] = jnp.sum(total, axis=0, keepdims=True)[:, :tokens]


def filter_grad(blocks, shards, channels, tokens):
    per = tokens // BLOCK
    rows = shards * per * channels
    return pl.pallas_call(
        functools.partial(filter_grad_kernel, shards, channels, tokens),
        out_shape=[
            jax.ShapeDtypeStruct((1, tokens), jnp.float32),
            pltpu.VMEM((4 * rows // shards * (shards + 1), LANES), jnp.bfloat16),
            pltpu.VMEM((8 * rows, LANES), jnp.bfloat16),
        ],
        in_specs=[pl.BlockSpec(memory_space=pltpu.VMEM)] * shards,
        out_specs=[pl.BlockSpec(memory_space=pltpu.VMEM)] * 3,
        scratch_shapes=[pltpu.VMEM((BLOCK, (per + 1) * BLOCK), jnp.float32)],
        compiler_params=pltpu.CompilerParams(vmem_limit_bytes=KERNEL_BYTES),
        cost_estimate=pl.CostEstimate(
            flops=2 * 3 * (per + 1) * rows * BLOCK * BLOCK, bytes_accessed=4 * rows * BLOCK * 2, transcendentals=0
        ),
        name="filter_grad",
    )(*blocks)


def convolve_block(held, me, tiles, channels, toe_high, toe_low, block, adjoint):
    count = 2 * tiles * channels
    lags = [block * tiles + n for n in range(tiles)]

    def window(lag):
        tile = me * tiles + lag if adjoint else (me + 1) * tiles - lag
        return held[pl.ds(pl.multiple_of(tile * 2 * channels, PACKED_ROWS), count), :]

    side = 0 if adjoint else 1
    left = jnp.concatenate([window(lag) for lag in lags], axis=1)
    pairs = [jnp.concatenate([toe_high[lag + 1], toe_low[lag + 1]], axis=side) for lag in lags]
    return dot(left, jnp.concatenate(pairs, axis=1 - side), 1, 1 - side)


def toeplitz_kernel(shards, channels, tokens, *refs):
    blocks, high_ref, low_ref, taps, skew = refs[:shards], *refs[shards:]
    me = lax.axis_index("context")
    tiles = tokens // LANES
    first = 2 * channels * tiles
    taps[0] = jnp.zeros((tiles, LANES), jnp.float32)
    for bits in range(shards):
        taps[(me ^ bits) + 1] = blocks[bits][first : first + tiles, :]
    high_ref[0] = jnp.zeros((LANES, LANES), jnp.bfloat16)
    low_ref[0] = jnp.zeros((LANES, LANES), jnp.bfloat16)
    width = (tiles + 1) * LANES

    for step in range(shards):
        last, sheet = taps[step], taps[step + 1]
        lines = [last[tiles - 1 : tiles, :]] + [sheet[n : n + 1, :] for n in range(tiles)]
        lean = jnp.concatenate([jnp.broadcast_to(line, (8, LANES)) for line in lines], axis=1)
        lean = pltpu.roll(lean, 0, 1, stride=1, stride_axis=0)
        skew[step] = lean

    def build(step, carry):
        skewed = skew[step]
        for group in range(LANES // PACKED_ROWS):
            top, bottom = (
                pltpu.roll(skewed, PACKED_ROWS * group + rows, 1) if group + rows else skewed
                for rows in (0, 8)
            )
            pair = halves(jnp.concatenate([top, bottom], axis=0))
            for ref, part in zip((high_ref, low_ref), pair):
                for tile in range(tiles):
                    ref[
                        step * tiles + tile + 1, group * PACKED_ROWS : (group + 1) * PACKED_ROWS, :
                    ] = part[:, (tile + 1) * LANES : (tile + 2) * LANES]
        return carry

    lax.fori_loop(0, shards, build, 0, unroll=min(4, shards))


def toeplitz_tiles(blocks, shards, channels, tokens):
    tiles = tokens // LANES
    shape = (shards * tiles + 1, LANES, LANES)
    return pl.pallas_call(
        functools.partial(toeplitz_kernel, shards, channels, tokens),
        out_shape=[pltpu.VMEM(shape, jnp.bfloat16)] * 2,
        in_specs=[pl.BlockSpec(memory_space=pltpu.VMEM)] * shards,
        out_specs=[pl.BlockSpec(memory_space=pltpu.VMEM)] * 2,
        scratch_shapes=[pltpu.VMEM((shards + 1, tiles, LANES), jnp.float32), pltpu.VMEM((shards, 8, (tiles + 1) * LANES), jnp.float32)],
        compiler_params=pltpu.CompilerParams(vmem_limit_bytes=KERNEL_BYTES),
        cost_estimate=pl.CostEstimate(
            flops=16 * shape[0] * LANES * LANES, bytes_accessed=4 * shape[0] * LANES * LANES, transcendentals=0
        ),
        name="toeplitz_tiles",
    )(*blocks)


def convolve_kernel(shards, channels, tokens, *refs):
    own_ref, sig, cot, toe_high, toe_low, gain_ref, out_ref, back_ref, conv, back = refs
    me = lax.axis_index("context")
    tiles = tokens // LANES

    def total(held, blocks, adjoint):
        parts = [
            convolve_block(held, me, tiles, channels, toe_high, toe_low, block, adjoint) for block in range(blocks)
        ]
        return sum(parts[1:], parts[0])

    def run(index):
        conv[...] = total(sig, index + 1, False)
        back[...] = total(cot, shards - index, True)

    for index in range(shards):
        pl.when(me == index)(functools.partial(run, index))
    factor = 1.0 / math.sqrt(shards * tokens)
    square_row = lax.broadcasted_iota(jnp.int32, (channels, channels), 0)
    square_lane = lax.broadcasted_iota(jnp.int32, (channels, channels), 1)
    gain = jnp.sum(
        jnp.where(square_row == square_lane, jnp.broadcast_to(gain_ref[...], (channels, channels)), 0.0),
        axis=1,
        keepdims=True,
    )
    for tile in range(tiles):
        lanes = slice(tile * LANES, (tile + 1) * LANES)
        for ref, value, first in ((out_ref, conv, 0), (back_ref, back, tiles)):
            own = own_ref[(first + tile) * channels : (first + tile + 1) * channels, :]
            top = tile * 2 * channels
            both = value[top : top + channels, :] + value[top + channels : top + 2 * channels, :]
            ref[:, lanes] = (both[:, :LANES] + both[:, LANES:]) * factor + gain * own


def convolve(own, held, toeplitz, skip_gain, shards, channels, tokens):
    count = 2 * channels * tokens // LANES
    return pl.pallas_call(
        functools.partial(convolve_kernel, shards, channels, tokens),
        out_shape=[pltpu.VMEM((channels, tokens), jnp.float32)] * 2,
        in_specs=[pl.BlockSpec(memory_space=pltpu.VMEM)] * 6,
        out_specs=[pl.BlockSpec(memory_space=pltpu.VMEM)] * 2,
        scratch_shapes=[pltpu.VMEM((count, 2 * LANES), jnp.float32)] * 2,
        compiler_params=pltpu.CompilerParams(vmem_limit_bytes=KERNEL_BYTES),
        cost_estimate=pl.CostEstimate(
            flops=2 * (shards + 1) * tokens * count * 2 * LANES,
            bytes_accessed=8 * shards * count * LANES,
            transcendentals=0,
        ),
        name="convolve",
    )(own, *held, *toeplitz, skip_gain.reshape(1, channels))


def finish_kernel(scale, value_ref, other_ref, output_ref, grad_ref, filter_out, output_out, grad_out):
    filter_out[...] = (value_ref[...] + other_ref[...]) * scale
    output_out[...] = output_ref[...]
    grad_out[...] = grad_ref[...]


def finish(value, other, output, grad_signal, scale):
    return pl.pallas_call(
        functools.partial(finish_kernel, scale),
        out_shape=[jax.ShapeDtypeStruct(x.shape, x.dtype) for x in (value, output, grad_signal)],
        in_specs=[pl.BlockSpec(memory_space=pltpu.VMEM)] * 4,
        out_specs=[pl.BlockSpec(memory_space=pltpu.VMEM)] * 3,
        compiler_params=pltpu.CompilerParams(vmem_limit_bytes=KERNEL_BYTES),
        name="finish",
    )(value, other, output, grad_signal)


def direct_body(signal, filter_taps, skip_gain, cotangent):
    shards, groups = lax.axis_size("context"), lax.axis_size("chan")
    channels, tokens = signal.shape
    stacked = stack_local(signal, cotangent, filter_taps)
    blocks = gather_blocks(stacked, shards)
    value, *held = filter_grad(blocks, shards, channels, tokens)
    toeplitz = toeplitz_tiles(blocks, shards, channels, tokens)
    other = None
    bits = 1
    while bits < groups:
        if other is not None:
            value = value + other
            value, *toeplitz = lax.optimization_barrier((value, *toeplitz))
        other = lax.ppermute(value, "chan", [(i, i ^ bits) for i in range(groups)])
        bits *= 2
    output, grad_signal = convolve(blocks[0], held, toeplitz, skip_gain, shards, channels, tokens)
    scale = 1.0 / math.sqrt(shards * tokens)
    grad_filter, output, grad_signal = finish(value, other, output, grad_signal, scale)
    return (output, grad_signal, grad_filter.reshape(tokens))


def rotation(first, second, period):
    turned = first * second % period
    return turned.astype(jnp.float32) * (2.0 * math.pi / period)


def table_product(real_part, imag_part, cosine, sine_table):
    return (
        real_part * cosine - imag_part * sine_table,
        real_part * sine_table + imag_part * cosine,
    )


def along_last(real_part, imag_part, angle_table):
    cosine = jnp.cos(angle_table)
    sine_table = jnp.sin(angle_table)
    new_real = jnp.matmul(real_part, cosine, precision=exact_mode) - jnp.matmul(
        imag_part, sine_table, precision=exact_mode
    )
    new_imag = jnp.matmul(real_part, sine_table, precision=exact_mode) + jnp.matmul(
        imag_part, cosine, precision=exact_mode
    )
    return (new_real, new_imag)


def along_slow(real_part, imag_part, angle_table):
    cosine = jnp.cos(angle_table)
    sine_table = jnp.sin(angle_table)
    new_real = jnp.einsum("gsjd,sa->gajd", real_part, cosine, precision=exact_mode) - jnp.einsum(
        "gsjd,sa->gajd", imag_part, sine_table, precision=exact_mode
    )
    new_imag = jnp.einsum(
        "gsjd,sa->gajd", real_part, sine_table, precision=exact_mode
    ) + jnp.einsum("gsjd,sa->gajd", imag_part, cosine, precision=exact_mode)
    return (new_real, new_imag)


def finish_sections(real_part, imag_part, stride, shards, length):
    sources = jnp.arange(shards, dtype=jnp.int32)
    slower = jnp.arange(stride, dtype=jnp.int32)
    slow_angle = -rotation(slower[:, None], slower[None, :], stride)
    real_part, imag_part = along_slow(real_part, imag_part, slow_angle)
    inner_twist = -rotation(slower[:, None, None], sources[None, None, :], length)
    real_part, imag_part = table_product(
        real_part, imag_part, jnp.cos(inner_twist), jnp.sin(inner_twist)
    )
    last_angle = -rotation(sources[:, None], sources[None, :], shards)
    return along_last(real_part, imag_part, last_angle)


def forward(stacked):
    shards = lax.axis_size("context")
    position = lax.axis_index("context")
    signals, length = stacked.shape
    stride = length // shards
    period = 2 * shards * length
    sources = jnp.arange(shards, dtype=jnp.int32)
    slower = jnp.arange(stride, dtype=jnp.int32)
    blocks = stacked.reshape(signals, stride, shards)
    columns = lax.all_to_all(blocks, "context", split_axis=2, concat_axis=2, tiled=True)
    token_ids = shards * slower[:, None] + position
    order = jnp.arange(2 * shards, dtype=jnp.int32)
    first_angle = -rotation(sources[:, None], order[None, :], 2 * shards)
    real_part = jnp.matmul(columns, jnp.cos(first_angle), precision=exact_mode)
    imag_part = jnp.matmul(columns, jnp.sin(first_angle), precision=exact_mode)
    twist = -rotation(token_ids, order[None, :], period)
    real_part, imag_part = table_product(real_part, imag_part, jnp.cos(twist), jnp.sin(twist))
    spectra = jnp.stack([real_part, imag_part]).reshape(2, signals, stride, 2, shards)
    spectra = lax.all_to_all(spectra, "context", split_axis=4, concat_axis=4, tiled=True)
    real_part, imag_part = finish_sections(spectra[0], spectra[1], stride, shards, length)
    return (real_part, imag_part, order)


def inverse(real_part, imag_part, order):
    shards = lax.axis_size("context")
    position = lax.axis_index("context")
    signals, stride = (real_part.shape[0], real_part.shape[1])
    length = stride * shards
    period = 2 * shards * length
    sources = jnp.arange(shards, dtype=jnp.int32)
    slower = jnp.arange(stride, dtype=jnp.int32)
    last_angle = rotation(sources[:, None], sources[None, :], shards)
    real_part, imag_part = along_last(real_part, imag_part, last_angle)
    inner_twist = rotation(slower[:, None, None], sources[None, None, :], length)
    real_part, imag_part = table_product(
        real_part, imag_part, jnp.cos(inner_twist), jnp.sin(inner_twist)
    )
    slow_angle = rotation(slower[:, None], slower[None, :], stride)
    real_part, imag_part = along_slow(real_part, imag_part, slow_angle)
    spectra = lax.all_to_all(
        jnp.stack([real_part, imag_part]), "context", split_axis=4, concat_axis=4, tiled=True
    )
    real_part = spectra[0].reshape(signals, stride, 2 * shards)
    imag_part = spectra[1].reshape(signals, stride, 2 * shards)
    token_ids = shards * slower[:, None] + position
    twist = rotation(token_ids, order[None, :], period)
    real_part, imag_part = table_product(real_part, imag_part, jnp.cos(twist), jnp.sin(twist))
    first_angle = rotation(order[:, None], sources[None, :], 2 * shards)
    cosine = jnp.cos(first_angle)
    sine_table = jnp.sin(first_angle)
    out_real = jnp.matmul(real_part, cosine, precision=exact_mode) - jnp.matmul(
        imag_part, sine_table, precision=exact_mode
    )
    out_imag = jnp.matmul(real_part, sine_table, precision=exact_mode) + jnp.matmul(
        imag_part, cosine, precision=exact_mode
    )
    results = jnp.stack([out_real, out_imag])
    blocks = lax.all_to_all(results, "context", split_axis=3, concat_axis=3, tiled=True)
    return blocks.reshape(blocks.shape[0], signals, length)


def transform_body(signal, filter_taps, skip_gain, cotangent):
    shards = lax.axis_size("context")
    channels, length = signal.shape
    factor = 1.0 / (2 * shards * length * math.sqrt(shards * length))
    stacked = jnp.concatenate([signal, cotangent, filter_taps[None, :]], axis=0)
    real_part, imag_part, order = forward(stacked)
    sig_re = real_part[:channels]
    sig_im = imag_part[:channels]
    cot_re = real_part[channels : 2 * channels]
    cot_im = imag_part[channels : 2 * channels]
    fil_re = real_part[2 * channels :]
    fil_im = imag_part[2 * channels :]
    out_re = sig_re * fil_re - sig_im * fil_im
    out_im = sig_re * fil_im + sig_im * fil_re
    back_re = cot_re * fil_re + cot_im * fil_im
    back_im = cot_im * fil_re - cot_re * fil_im
    grad_re = jnp.sum(cot_re * sig_re + cot_im * sig_im, axis=0, keepdims=True)
    grad_im = jnp.sum(cot_im * sig_re - cot_re * sig_im, axis=0, keepdims=True)
    restored = inverse(
        jnp.concatenate([out_re - back_im, grad_re], axis=0),
        jnp.concatenate([out_im + back_re, grad_im], axis=0),
        order,
    )
    conv_out = restored[0, :channels]
    conv_back = restored[1, :channels]
    partial_value = restored[0, channels]
    output = conv_out * factor + skip_gain[:, None] * signal
    grad_signal = conv_back * factor + skip_gain[:, None] * cotangent
    grad_filter = lax.psum(partial_value * factor, "chan")
    return (output, grad_signal, grad_filter)


def fits_direct(channels, tokens, shards):
    held = 4 * shards * tokens * (2 * channels + 1)
    scratch = 16 * shards * tokens * channels + 4 * (shards * tokens + LANES) * LANES
    groups = lax.axis_size("chan")
    whole = groups & (groups - 1) == 0 and channels % PACKED_ROWS == 0 and tokens % (8 * LANES) == 0 and shards & (shards - 1) == 0
    return whole and shards > 1 and 2 * held + scratch < KERNEL_BYTES


def body(signal, filter_taps, skip_gain, cotangent):
    channels, tokens = signal.shape
    if fits_direct(channels, tokens, lax.axis_size("context")):
        return direct_body(signal, filter_taps, skip_gain, cotangent)
    return transform_body(signal, filter_taps, skip_gain, cotangent)


def solution(mesh):
    return jax.shard_map(
        body,
        mesh=mesh,
        in_specs=(P("chan", "context"), P("context"), P("chan"), P("chan", "context")),
        out_specs=(P("chan", "context"), P("chan", "context"), P("context")),
        check_vma=False,
    )
```

```python
import functools
import math

import jax
import jax.numpy as jnp
from jax import lax
from jax.experimental import pallas as pl
from jax.experimental.pallas import tpu as pltpu
from jax.sharding import PartitionSpec as P

exact_mode = lax.Precision.HIGHEST

SHARDS = 8
FLIPS = ((0, 0), (2, 4), (6, 6), (4, 2))
LANES = 128
BLOCK = 256
PACKED_ROWS = 16
KERNEL_BYTES = 16 * 1024 * 1024


def halves(value):
    high = value.astype(jnp.bfloat16)
    low = (value - high.astype(jnp.float32)).astype(jnp.bfloat16)
    return high, low


def dot(left, right, left_dim, right_dim):
    return lax.dot_general(
        left, right, (((left_dim,), (right_dim,)), ((), ())), preferred_element_type=jnp.float32
    )


def stack_kernel(signal_ref, cotangent_ref, taps_ref, out_ref):
    channels, tokens = signal_ref.shape
    row = 0
    for source in (signal_ref, cotangent_ref):
        for tile in range(tokens // LANES):
            out_ref[row : row + channels, :] = source[:, tile * LANES : (tile + 1) * LANES]
            row += channels
    out_ref[row:, :] = taps_ref[...]


def stack_local(signal, cotangent, taps):
    channels, tokens = signal.shape
    rows = (2 * channels * tokens + tokens) // LANES
    return pl.pallas_call(
        stack_kernel,
        out_shape=pltpu.VMEM((rows, LANES), jnp.float32),
        in_specs=[pl.BlockSpec(memory_space=pltpu.VMEM)] * 3,
        out_specs=pl.BlockSpec(memory_space=pltpu.VMEM),
        name="stack_local",
    )(signal, cotangent, taps.reshape(tokens // LANES, LANES))


def source_index(me, entry):
    core = me % 2 if entry % 2 == 0 else 1 - me % 2
    even, odd = FLIPS[entry // 2]
    return me ^ (even + (odd - even) * core + entry % 2)


def gather_blocks(stacked):
    def fetched(value, entry):
        return lax.ppermute(value, "context", [(source_index(i, entry), i) for i in range(SHARDS)])

    found = {0: stacked}
    for entry in range(2, SHARDS, 2):
        found[entry] = fetched(stacked, entry)
    for entry in range(0, SHARDS, 2):
        found[entry + 1] = fetched(found[entry], 1)
    return [found[entry] for entry in range(SHARDS)]


def place_rows(block_ref, first, index, channels, tokens, ref, start):
    tiles = tokens // LANES
    for tile in range(tiles):
        rows = first + tile * channels
        both = jnp.concatenate(halves(block_ref[rows : rows + channels, :]), axis=0)
        at = pl.multiple_of((index * tiles + tile) * 2 * channels + start, PACKED_ROWS)
        ref[pl.ds(at, 2 * channels), :] = both


def paired_tiles(ref, start, count, channels, half):
    def rows(tile):
        at = pl.multiple_of((start + tile) * 2 * channels + half * channels, PACKED_ROWS)
        return ref[pl.ds(at, channels), :]

    return jnp.concatenate(
        [jnp.concatenate([rows(tile), rows(tile + 1)], axis=1) for tile in range(0, count, 2)], axis=0
    )


def filter_grad_kernel(shards, channels, tokens, *refs):
    blocks, out_ref, sig, cot, folded = refs[:shards], *refs[shards:]
    me = lax.axis_index("context")
    per, tiles = tokens // BLOCK, tokens // LANES
    count = 2 * tiles * channels
    rows = shards * count
    sig[:count, :] = jnp.zeros((count, LANES), jnp.bfloat16)
    cot[rows:, :] = jnp.zeros((rows, LANES), jnp.bfloat16)
    for bits in range(shards):
        index = source_index(me, bits)
        place_rows(blocks[bits], 0, index, channels, tokens, sig, count)
        place_rows(blocks[bits], channels * tiles, index, channels, tokens, cot, 0)
    held = [paired_tiles(sig, tiles, shards * tiles, channels, half) for half in range(2)]
    for lag in range(per + 1):
        window = [
            paired_tiles(cot, me * tiles + 2 * lag, shards * tiles, channels, half) for half in range(2)
        ]
        folded[:, lag * BLOCK : (lag + 1) * BLOCK] = dot(jnp.concatenate([held[0], held[0], held[1]], axis=0), jnp.concatenate([window[0], window[1], window[0]], axis=0), 0, 0)
    width = (per + 1) * BLOCK - LANES
    total = None
    for group in range(LANES // 8):
        part = (
            folded[8 * group : 8 * group + 8, :width]
            + folded[LANES + 8 * group : LANES + 8 * group + 8, LANES:]
        )
        if group:
            part = pltpu.roll(part, width - 8 * group, 1)
        total = part if total is None else total + part
    row = lax.broadcasted_iota(jnp.int32, total.shape, 0)
    for step in (1, 2, 4):
        total = jnp.where((row & step) != 0, pltpu.roll(total, width - step, 1), total)
    out_ref[...] = jnp.sum(total, axis=0, keepdims=True)[:, :tokens]


def filter_grad(blocks, shards, channels, tokens):
    per = tokens // BLOCK
    rows = shards * per * channels
    return pl.pallas_call(
        functools.partial(filter_grad_kernel, shards, channels, tokens),
        out_shape=[
            jax.ShapeDtypeStruct((1, tokens), jnp.float32),
            pltpu.VMEM((4 * rows // shards * (shards + 1), LANES), jnp.bfloat16),
            pltpu.VMEM((8 * rows, LANES), jnp.bfloat16),
        ],
        in_specs=[pl.BlockSpec(memory_space=pltpu.VMEM)] * shards,
        out_specs=[pl.BlockSpec(memory_space=pltpu.VMEM)] * 3,
        scratch_shapes=[pltpu.VMEM((BLOCK, (per + 1) * BLOCK), jnp.float32)],
        compiler_params=pltpu.CompilerParams(vmem_limit_bytes=KERNEL_BYTES),
        cost_estimate=pl.CostEstimate(
            flops=2 * 3 * (per + 1) * rows * BLOCK * BLOCK, bytes_accessed=4 * rows * BLOCK * 2, transcendentals=0
        ),
        name="filter_grad",
    )(*blocks)


def convolve_block(held, me, tiles, channels, toe_high, toe_low, block, adjoint):
    count = 2 * tiles * channels
    lags = [block * tiles + n for n in range(tiles)]

    def window(lag):
        tile = me * tiles + lag if adjoint else (me + 1) * tiles - lag
        return held[pl.ds(pl.multiple_of(tile * 2 * channels, PACKED_ROWS), count), :]

    side = 0 if adjoint else 1
    left = jnp.concatenate([window(lag) for lag in lags], axis=1)
    pairs = [jnp.concatenate([toe_high[lag + 1], toe_low[lag + 1]], axis=side) for lag in lags]
    return dot(left, jnp.concatenate(pairs, axis=1 - side), 1, 1 - side)


def toeplitz_kernel(shards, channels, tokens, *refs):
    blocks, high_ref, low_ref, taps, skew = refs[:shards], *refs[shards:]
    me = lax.axis_index("context")
    tiles = tokens // LANES
    first = 2 * channels * tiles
    taps[0] = jnp.zeros((tiles, LANES), jnp.float32)
    for bits in range(shards):
        taps[source_index(me, bits) + 1] = blocks[bits][first : first + tiles, :]
    high_ref[0] = jnp.zeros((LANES, LANES), jnp.bfloat16)
    low_ref[0] = jnp.zeros((LANES, LANES), jnp.bfloat16)
    width = (tiles + 1) * LANES

    for step in range(shards):
        last, sheet = taps[step], taps[step + 1]
        lines = [last[tiles - 1 : tiles, :]] + [sheet[n : n + 1, :] for n in range(tiles)]
        lean = jnp.concatenate([jnp.broadcast_to(line, (8, LANES)) for line in lines], axis=1)
        lean = pltpu.roll(lean, 0, 1, stride=1, stride_axis=0)
        skew[step] = lean

    def build(step, carry):
        skewed = skew[step]
        for group in range(LANES // PACKED_ROWS):
            top, bottom = (
                pltpu.roll(skewed, PACKED_ROWS * group + rows, 1) if group + rows else skewed
                for rows in (0, 8)
            )
            pair = halves(jnp.concatenate([top, bottom], axis=0))
            for ref, part in zip((high_ref, low_ref), pair):
                for tile in range(tiles):
                    ref[
                        step * tiles + tile + 1, group * PACKED_ROWS : (group + 1) * PACKED_ROWS, :
                    ] = part[:, (tile + 1) * LANES : (tile + 2) * LANES]
        return carry

    lax.fori_loop(0, shards, build, 0, unroll=min(4, shards))


def toeplitz_tiles(blocks, shards, channels, tokens):
    tiles = tokens // LANES
    shape = (shards * tiles + 1, LANES, LANES)
    return pl.pallas_call(
        functools.partial(toeplitz_kernel, shards, channels, tokens),
        out_shape=[pltpu.VMEM(shape, jnp.bfloat16)] * 2,
        in_specs=[pl.BlockSpec(memory_space=pltpu.VMEM)] * shards,
        out_specs=[pl.BlockSpec(memory_space=pltpu.VMEM)] * 2,
        scratch_shapes=[pltpu.VMEM((shards + 1, tiles, LANES), jnp.float32), pltpu.VMEM((shards, 8, (tiles + 1) * LANES), jnp.float32)],
        compiler_params=pltpu.CompilerParams(vmem_limit_bytes=KERNEL_BYTES),
        cost_estimate=pl.CostEstimate(
            flops=16 * shape[0] * LANES * LANES, bytes_accessed=4 * shape[0] * LANES * LANES, transcendentals=0
        ),
        name="toeplitz_tiles",
    )(*blocks)


def convolve_kernel(shards, channels, tokens, *refs):
    own_ref, sig, cot, toe_high, toe_low, gain_ref, out_ref, back_ref, conv, back = refs
    me = lax.axis_index("context")
    tiles = tokens // LANES

    def total(held, blocks, adjoint):
        parts = [
            convolve_block(held, me, tiles, channels, toe_high, toe_low, block, adjoint) for block in range(blocks)
        ]
        return sum(parts[1:], parts[0])

    def run(index):
        conv[...] = total(sig, index + 1, False)
        back[...] = total(cot, shards - index, True)

    for index in range(shards):
        pl.when(me == index)(functools.partial(run, index))
    factor = 1.0 / math.sqrt(shards * tokens)
    square_row = lax.broadcasted_iota(jnp.int32, (channels, channels), 0)
    square_lane = lax.broadcasted_iota(jnp.int32, (channels, channels), 1)
    gain = jnp.sum(
        jnp.where(square_row == square_lane, jnp.broadcast_to(gain_ref[...], (channels, channels)), 0.0),
        axis=1,
        keepdims=True,
    )
    for tile in range(tiles):
        lanes = slice(tile * LANES, (tile + 1) * LANES)
        for ref, value, first in ((out_ref, conv, 0), (back_ref, back, tiles)):
            own = own_ref[(first + tile) * channels : (first + tile + 1) * channels, :]
            top = tile * 2 * channels
            both = value[top : top + channels, :] + value[top + channels : top + 2 * channels, :]
            ref[:, lanes] = (both[:, :LANES] + both[:, LANES:]) * factor + gain * own


def convolve(own, held, toeplitz, skip_gain, shards, channels, tokens):
    count = 2 * channels * tokens // LANES
    return pl.pallas_call(
        functools.partial(convolve_kernel, shards, channels, tokens),
        out_shape=[pltpu.VMEM((channels, tokens), jnp.float32)] * 2,
        in_specs=[pl.BlockSpec(memory_space=pltpu.VMEM)] * 6,
        out_specs=[pl.BlockSpec(memory_space=pltpu.VMEM)] * 2,
        scratch_shapes=[pltpu.VMEM((count, 2 * LANES), jnp.float32)] * 2,
        compiler_params=pltpu.CompilerParams(vmem_limit_bytes=KERNEL_BYTES),
        cost_estimate=pl.CostEstimate(
            flops=2 * (shards + 1) * tokens * count * 2 * LANES,
            bytes_accessed=8 * shards * count * LANES,
            transcendentals=0,
        ),
        name="convolve",
    )(own, *held, *toeplitz, skip_gain.reshape(1, channels))


def finish_kernel(scale, value_ref, other_ref, output_ref, grad_ref, filter_out, output_out, grad_out):
    filter_out[...] = (value_ref[...] + other_ref[...]) * scale
    output_out[...] = output_ref[...]
    grad_out[...] = grad_ref[...]


def finish(value, other, output, grad_signal, scale):
    return pl.pallas_call(
        functools.partial(finish_kernel, scale),
        out_shape=[jax.ShapeDtypeStruct(x.shape, x.dtype) for x in (value, output, grad_signal)],
        in_specs=[pl.BlockSpec(memory_space=pltpu.VMEM)] * 4,
        out_specs=[pl.BlockSpec(memory_space=pltpu.VMEM)] * 3,
        compiler_params=pltpu.CompilerParams(vmem_limit_bytes=KERNEL_BYTES),
        name="finish",
    )(value, other, output, grad_signal)


def direct_body(signal, filter_taps, skip_gain, cotangent):
    shards, groups = lax.axis_size("context"), lax.axis_size("chan")
    channels, tokens = signal.shape
    stacked = stack_local(signal, cotangent, filter_taps)
    blocks = gather_blocks(stacked)
    value, *held = filter_grad(blocks, shards, channels, tokens)
    toeplitz = toeplitz_tiles(blocks, shards, channels, tokens)
    other = None
    bits = 1
    while bits < groups:
        if other is not None:
            value = value + other
            value, *toeplitz = lax.optimization_barrier((value, *toeplitz))
        other = lax.ppermute(value, "chan", [(i, i ^ bits) for i in range(groups)])
        bits *= 2
    output, grad_signal = convolve(blocks[0], held, toeplitz, skip_gain, shards, channels, tokens)
    scale = 1.0 / math.sqrt(shards * tokens)
    grad_filter, output, grad_signal = finish(value, other, output, grad_signal, scale)
    return (output, grad_signal, grad_filter.reshape(tokens))


def rotation(first, second, period):
    turned = first * second % period
    return turned.astype(jnp.float32) * (2.0 * math.pi / period)


def table_product(real_part, imag_part, cosine, sine_table):
    return (
        real_part * cosine - imag_part * sine_table,
        real_part * sine_table + imag_part * cosine,
    )


def along_last(real_part, imag_part, angle_table):
    cosine = jnp.cos(angle_table)
    sine_table = jnp.sin(angle_table)
    new_real = jnp.matmul(real_part, cosine, precision=exact_mode) - jnp.matmul(
        imag_part, sine_table, precision=exact_mode
    )
    new_imag = jnp.matmul(real_part, sine_table, precision=exact_mode) + jnp.matmul(
        imag_part, cosine, precision=exact_mode
    )
    return (new_real, new_imag)


def along_slow(real_part, imag_part, angle_table):
    cosine = jnp.cos(angle_table)
    sine_table = jnp.sin(angle_table)
    new_real = jnp.einsum("gsjd,sa->gajd", real_part, cosine, precision=exact_mode) - jnp.einsum(
        "gsjd,sa->gajd", imag_part, sine_table, precision=exact_mode
    )
    new_imag = jnp.einsum(
        "gsjd,sa->gajd", real_part, sine_table, precision=exact_mode
    ) + jnp.einsum("gsjd,sa->gajd", imag_part, cosine, precision=exact_mode)
    return (new_real, new_imag)


def finish_sections(real_part, imag_part, stride, shards, length):
    sources = jnp.arange(shards, dtype=jnp.int32)
    slower = jnp.arange(stride, dtype=jnp.int32)
    slow_angle = -rotation(slower[:, None], slower[None, :], stride)
    real_part, imag_part = along_slow(real_part, imag_part, slow_angle)
    inner_twist = -rotation(slower[:, None, None], sources[None, None, :], length)
    real_part, imag_part = table_product(
        real_part, imag_part, jnp.cos(inner_twist), jnp.sin(inner_twist)
    )
    last_angle = -rotation(sources[:, None], sources[None, :], shards)
    return along_last(real_part, imag_part, last_angle)


def forward(stacked):
    shards = lax.axis_size("context")
    position = lax.axis_index("context")
    signals, length = stacked.shape
    stride = length // shards
    period = 2 * shards * length
    sources = jnp.arange(shards, dtype=jnp.int32)
    slower = jnp.arange(stride, dtype=jnp.int32)
    blocks = stacked.reshape(signals, stride, shards)
    columns = lax.all_to_all(blocks, "context", split_axis=2, concat_axis=2, tiled=True)
    token_ids = shards * slower[:, None] + position
    order = jnp.arange(2 * shards, dtype=jnp.int32)
    first_angle = -rotation(sources[:, None], order[None, :], 2 * shards)
    real_part = jnp.matmul(columns, jnp.cos(first_angle), precision=exact_mode)
    imag_part = jnp.matmul(columns, jnp.sin(first_angle), precision=exact_mode)
    twist = -rotation(token_ids, order[None, :], period)
    real_part, imag_part = table_product(real_part, imag_part, jnp.cos(twist), jnp.sin(twist))
    spectra = jnp.stack([real_part, imag_part]).reshape(2, signals, stride, 2, shards)
    spectra = lax.all_to_all(spectra, "context", split_axis=4, concat_axis=4, tiled=True)
    real_part, imag_part = finish_sections(spectra[0], spectra[1], stride, shards, length)
    return (real_part, imag_part, order)


def inverse(real_part, imag_part, order):
    shards = lax.axis_size("context")
    position = lax.axis_index("context")
    signals, stride = (real_part.shape[0], real_part.shape[1])
    length = stride * shards
    period = 2 * shards * length
    sources = jnp.arange(shards, dtype=jnp.int32)
    slower = jnp.arange(stride, dtype=jnp.int32)
    last_angle = rotation(sources[:, None], sources[None, :], shards)
    real_part, imag_part = along_last(real_part, imag_part, last_angle)
    inner_twist = rotation(slower[:, None, None], sources[None, None, :], length)
    real_part, imag_part = table_product(
        real_part, imag_part, jnp.cos(inner_twist), jnp.sin(inner_twist)
    )
    slow_angle = rotation(slower[:, None], slower[None, :], stride)
    real_part, imag_part = along_slow(real_part, imag_part, slow_angle)
    spectra = lax.all_to_all(
        jnp.stack([real_part, imag_part]), "context", split_axis=4, concat_axis=4, tiled=True
    )
    real_part = spectra[0].reshape(signals, stride, 2 * shards)
    imag_part = spectra[1].reshape(signals, stride, 2 * shards)
    token_ids = shards * slower[:, None] + position
    twist = rotation(token_ids, order[None, :], period)
    real_part, imag_part = table_product(real_part, imag_part, jnp.cos(twist), jnp.sin(twist))
    first_angle = rotation(order[:, None], sources[None, :], 2 * shards)
    cosine = jnp.cos(first_angle)
    sine_table = jnp.sin(first_angle)
    out_real = jnp.matmul(real_part, cosine, precision=exact_mode) - jnp.matmul(
        imag_part, sine_table, precision=exact_mode
    )
    out_imag = jnp.matmul(real_part, sine_table, precision=exact_mode) + jnp.matmul(
        imag_part, cosine, precision=exact_mode
    )
    results = jnp.stack([out_real, out_imag])
    blocks = lax.all_to_all(results, "context", split_axis=3, concat_axis=3, tiled=True)
    return blocks.reshape(blocks.shape[0], signals, length)


def transform_body(signal, filter_taps, skip_gain, cotangent):
    shards = lax.axis_size("context")
    channels, length = signal.shape
    factor = 1.0 / (2 * shards * length * math.sqrt(shards * length))
    stacked = jnp.concatenate([signal, cotangent, filter_taps[None, :]], axis=0)
    real_part, imag_part, order = forward(stacked)
    sig_re = real_part[:channels]
    sig_im = imag_part[:channels]
    cot_re = real_part[channels : 2 * channels]
    cot_im = imag_part[channels : 2 * channels]
    fil_re = real_part[2 * channels :]
    fil_im = imag_part[2 * channels :]
    out_re = sig_re * fil_re - sig_im * fil_im
    out_im = sig_re * fil_im + sig_im * fil_re
    back_re = cot_re * fil_re + cot_im * fil_im
    back_im = cot_im * fil_re - cot_re * fil_im
    grad_re = jnp.sum(cot_re * sig_re + cot_im * sig_im, axis=0, keepdims=True)
    grad_im = jnp.sum(cot_im * sig_re - cot_re * sig_im, axis=0, keepdims=True)
    restored = inverse(
        jnp.concatenate([out_re - back_im, grad_re], axis=0),
        jnp.concatenate([out_im + back_re, grad_im], axis=0),
        order,
    )
    conv_out = restored[0, :channels]
    conv_back = restored[1, :channels]
    partial_value = restored[0, channels]
    output = conv_out * factor + skip_gain[:, None] * signal
    grad_signal = conv_back * factor + skip_gain[:, None] * cotangent
    grad_filter = lax.psum(partial_value * factor, "chan")
    return (output, grad_signal, grad_filter)


def fits_direct(channels, tokens, shards):
    held = 4 * shards * tokens * (2 * channels + 1)
    scratch = 16 * shards * tokens * channels + 4 * (shards * tokens + LANES) * LANES
    groups = lax.axis_size("chan")
    whole = groups & (groups - 1) == 0 and channels % PACKED_ROWS == 0 and tokens % (8 * LANES) == 0 and shards & (shards - 1) == 0
    return whole and shards == SHARDS and 2 * held + scratch < KERNEL_BYTES


def body(signal, filter_taps, skip_gain, cotangent):
    channels, tokens = signal.shape
    if fits_direct(channels, tokens, lax.axis_size("context")):
        return direct_body(signal, filter_taps, skip_gain, cotangent)
    return transform_body(signal, filter_taps, skip_gain, cotangent)


def solution(mesh):
    return jax.shard_map(
        body,
        mesh=mesh,
        in_specs=(P("chan", "context"), P("context"), P("chan"), P("chan", "context")),
        out_specs=(P("chan", "context"), P("chan", "context"), P("context")),
        check_vma=False,
    )
```

```python
import functools
import math

import jax
import jax.numpy as jnp
from jax import lax
from jax.experimental import pallas as pl
from jax.experimental.pallas import tpu as pltpu
from jax.sharding import PartitionSpec as P

exact_mode = lax.Precision.HIGHEST

SHARDS = 8
FLIPS = ((0, 0), (2, 4), (6, 6), (4, 2))
LANES = 128
BLOCK = 256
PACKED_ROWS = 16
KERNEL_BYTES = 16 * 1024 * 1024


def halves(value):
    high = value.astype(jnp.bfloat16)
    low = (value - high.astype(jnp.float32)).astype(jnp.bfloat16)
    return high, low


def dot(left, right, left_dim, right_dim):
    return lax.dot_general(
        left, right, (((left_dim,), (right_dim,)), ((), ())), preferred_element_type=jnp.float32
    )


def stack_kernel(signal_ref, cotangent_ref, taps_ref, out_ref):
    channels, tokens = signal_ref.shape
    row = 0
    for source in (signal_ref, cotangent_ref):
        for tile in range(tokens // LANES):
            out_ref[row : row + channels, :] = source[:, tile * LANES : (tile + 1) * LANES]
            row += channels
    out_ref[row:, :] = taps_ref[...]


def stack_local(signal, cotangent, taps):
    channels, tokens = signal.shape
    rows = (2 * channels * tokens + tokens) // LANES
    return pl.pallas_call(
        stack_kernel,
        out_shape=pltpu.VMEM((rows, LANES), jnp.float32),
        in_specs=[pl.BlockSpec(memory_space=pltpu.VMEM)] * 3,
        out_specs=pl.BlockSpec(memory_space=pltpu.VMEM),
        name="stack_local",
    )(signal, cotangent, taps.reshape(tokens // LANES, LANES))


def source_index(me, entry):
    core = me % 2 if entry % 2 == 0 else 1 - me % 2
    even, odd = FLIPS[entry // 2]
    return me ^ (even + (odd - even) * core + entry % 2)


def gather_blocks(stacked):
    def fetched(value, entry):
        return lax.ppermute(value, "context", [(source_index(i, entry), i) for i in range(SHARDS)])

    found = {0: stacked}
    for entry in range(2, SHARDS, 2):
        found[entry] = fetched(stacked, entry)
    for entry in range(0, SHARDS, 2):
        found[entry + 1] = fetched(found[entry], 1)
    return [found[entry] for entry in range(SHARDS)]


def place_rows(block_ref, first, index, channels, tokens, ref, start):
    tiles = tokens // LANES
    for tile in range(tiles):
        rows = first + tile * channels
        both = jnp.concatenate(halves(block_ref[rows : rows + channels, :]), axis=0)
        at = pl.multiple_of((index * tiles + tile) * 2 * channels + start, PACKED_ROWS)
        ref[pl.ds(at, 2 * channels), :] = both


def paired_tiles(ref, start, count, channels, half):
    def rows(tile):
        at = pl.multiple_of((start + tile) * 2 * channels + half * channels, PACKED_ROWS)
        return ref[pl.ds(at, channels), :]

    return jnp.concatenate(
        [jnp.concatenate([rows(tile), rows(tile + 1)], axis=1) for tile in range(0, count, 2)], axis=0
    )


def filter_grad_kernel(shards, channels, tokens, *refs):
    blocks, out_ref, sig, cot, folded = refs[:shards], *refs[shards:]
    me = lax.axis_index("context")
    per, tiles = tokens // BLOCK, tokens // LANES
    count = 2 * tiles * channels
    rows = shards * count
    sig[:count, :] = jnp.zeros((count, LANES), jnp.bfloat16)
    cot[rows:, :] = jnp.zeros((rows, LANES), jnp.bfloat16)
    for bits in range(shards):
        index = source_index(me, bits)
        place_rows(blocks[bits], 0, index, channels, tokens, sig, count)
        place_rows(blocks[bits], channels * tiles, index, channels, tokens, cot, 0)
    held = [paired_tiles(sig, tiles, shards * tiles, channels, half) for half in range(2)]
    for lag in range(per + 1):
        window = [
            paired_tiles(cot, me * tiles + 2 * lag, shards * tiles, channels, half) for half in range(2)
        ]
        folded[:, lag * BLOCK : (lag + 1) * BLOCK] = dot(jnp.concatenate([held[0], held[0], held[1]], axis=0), jnp.concatenate([window[0], window[1], window[0]], axis=0), 0, 0)
    width = (per + 1) * BLOCK - LANES
    total = None
    for group in range(LANES // 8):
        part = (
            folded[8 * group : 8 * group + 8, :width]
            + folded[LANES + 8 * group : LANES + 8 * group + 8, LANES:]
        )
        if group:
            part = pltpu.roll(part, width - 8 * group, 1)
        total = part if total is None else total + part
    row = lax.broadcasted_iota(jnp.int32, total.shape, 0)
    for step in (1, 2, 4):
        total = jnp.where((row & step) != 0, pltpu.roll(total, width - step, 1), total)
    out_ref[...] = jnp.sum(total, axis=0, keepdims=True)[:, :tokens]


def filter_grad(blocks, shards, channels, tokens):
    per = tokens // BLOCK
    rows = shards * per * channels
    return pl.pallas_call(
        functools.partial(filter_grad_kernel, shards, channels, tokens),
        out_shape=[
            jax.ShapeDtypeStruct((1, tokens), jnp.float32),
            pltpu.VMEM((4 * rows // shards * (shards + 1), LANES), jnp.bfloat16),
            pltpu.VMEM((8 * rows, LANES), jnp.bfloat16),
        ],
        in_specs=[pl.BlockSpec(memory_space=pltpu.VMEM)] * shards,
        out_specs=[pl.BlockSpec(memory_space=pltpu.VMEM)] * 3,
        scratch_shapes=[pltpu.VMEM((BLOCK, (per + 1) * BLOCK), jnp.float32)],
        compiler_params=pltpu.CompilerParams(vmem_limit_bytes=KERNEL_BYTES),
        cost_estimate=pl.CostEstimate(
            flops=2 * 3 * (per + 1) * rows * BLOCK * BLOCK, bytes_accessed=4 * rows * BLOCK * 2, transcendentals=0
        ),
        name="filter_grad",
    )(*blocks)


def convolve_block(held, me, tiles, channels, toe_high, toe_low, block, adjoint):
    count = 2 * tiles * channels
    lags = [block * tiles + n for n in range(tiles)]

    def window(lag):
        tile = me * tiles + lag if adjoint else (me + 1) * tiles - lag
        return held[pl.ds(pl.multiple_of(tile * 2 * channels, PACKED_ROWS), count), :]

    side = 0 if adjoint else 1
    left = jnp.concatenate([window(lag) for lag in lags], axis=1)
    pairs = [jnp.concatenate([toe_high[lag + 1], toe_low[lag + 1]], axis=side) for lag in lags]
    return dot(left, jnp.concatenate(pairs, axis=1 - side), 1, 1 - side)


def toeplitz_kernel(shards, channels, tokens, *refs):
    blocks, high_ref, low_ref, taps, skew = refs[:shards], *refs[shards:]
    me = lax.axis_index("context")
    tiles = tokens // LANES
    first = 2 * channels * tiles
    taps[0] = jnp.zeros((tiles, LANES), jnp.float32)
    for bits in range(shards):
        taps[source_index(me, bits) + 1] = blocks[bits][first : first + tiles, :]
    high_ref[0] = jnp.zeros((LANES, LANES), jnp.bfloat16)
    low_ref[0] = jnp.zeros((LANES, LANES), jnp.bfloat16)
    width = (tiles + 1) * LANES

    for step in range(shards):
        last, sheet = taps[step], taps[step + 1]
        lines = [last[tiles - 1 : tiles, :]] + [sheet[n : n + 1, :] for n in range(tiles)]
        lean = jnp.concatenate([jnp.broadcast_to(line, (8, LANES)) for line in lines], axis=1)
        lean = pltpu.roll(lean, 0, 1, stride=1, stride_axis=0)
        skew[step] = lean

    def build(step, carry):
        skewed = skew[step]
        for group in range(LANES // PACKED_ROWS):
            top, bottom = (
                pltpu.roll(skewed, PACKED_ROWS * group + rows, 1) if group + rows else skewed
                for rows in (0, 8)
            )
            pair = halves(jnp.concatenate([top, bottom], axis=0))
            for ref, part in zip((high_ref, low_ref), pair):
                for tile in range(tiles):
                    ref[
                        step * tiles + tile + 1, group * PACKED_ROWS : (group + 1) * PACKED_ROWS, :
                    ] = part[:, (tile + 1) * LANES : (tile + 2) * LANES]
        return carry

    lax.fori_loop(0, shards, build, 0, unroll=min(4, shards))


def toeplitz_tiles(blocks, shards, channels, tokens):
    tiles = tokens // LANES
    shape = (shards * tiles + 1, LANES, LANES)
    return pl.pallas_call(
        functools.partial(toeplitz_kernel, shards, channels, tokens),
        out_shape=[pltpu.VMEM(shape, jnp.bfloat16)] * 2,
        in_specs=[pl.BlockSpec(memory_space=pltpu.VMEM)] * shards,
        out_specs=[pl.BlockSpec(memory_space=pltpu.VMEM)] * 2,
        scratch_shapes=[pltpu.VMEM((shards + 1, tiles, LANES), jnp.float32), pltpu.VMEM((shards, 8, (tiles + 1) * LANES), jnp.float32)],
        compiler_params=pltpu.CompilerParams(vmem_limit_bytes=KERNEL_BYTES),
        cost_estimate=pl.CostEstimate(
            flops=16 * shape[0] * LANES * LANES, bytes_accessed=4 * shape[0] * LANES * LANES, transcendentals=0
        ),
        name="toeplitz_tiles",
    )(*blocks)


def convolve_kernel(shards, channels, tokens, *refs):
    own_ref, sig, cot, toe_high, toe_low, gain_ref, out_ref, back_ref, conv, back = refs
    me = lax.axis_index("context")
    tiles = tokens // LANES

    def total(held, blocks, adjoint):
        parts = [
            convolve_block(held, me, tiles, channels, toe_high, toe_low, block, adjoint) for block in range(blocks)
        ]
        return sum(parts[1:], parts[0])

    def run(index):
        conv[...] = total(sig, index + 1, False)
        back[...] = total(cot, shards - index, True)

    for index in range(shards):
        pl.when(me == index)(functools.partial(run, index))
    factor = 1.0 / math.sqrt(shards * tokens)
    square_row = lax.broadcasted_iota(jnp.int32, (channels, channels), 0)
    square_lane = lax.broadcasted_iota(jnp.int32, (channels, channels), 1)
    gain = jnp.sum(
        jnp.where(square_row == square_lane, jnp.broadcast_to(gain_ref[...], (channels, channels)), 0.0),
        axis=1,
        keepdims=True,
    )
    for tile in range(tiles):
        lanes = slice(tile * LANES, (tile + 1) * LANES)
        for ref, value, first in ((out_ref, conv, 0), (back_ref, back, tiles)):
            own = own_ref[(first + tile) * channels : (first + tile + 1) * channels, :]
            top = tile * 2 * channels
            both = value[top : top + channels, :] + value[top + channels : top + 2 * channels, :]
            ref[:, lanes] = (both[:, :LANES] + both[:, LANES:]) * factor + gain * own


def convolve(own, held, toeplitz, skip_gain, shards, channels, tokens):
    count = 2 * channels * tokens // LANES
    return pl.pallas_call(
        functools.partial(convolve_kernel, shards, channels, tokens),
        out_shape=[pltpu.VMEM((channels, tokens), jnp.float32)] * 2,
        in_specs=[pl.BlockSpec(memory_space=pltpu.VMEM)] * 6,
        out_specs=[pl.BlockSpec(memory_space=pltpu.VMEM)] * 2,
        scratch_shapes=[pltpu.VMEM((count, 2 * LANES), jnp.float32)] * 2,
        compiler_params=pltpu.CompilerParams(vmem_limit_bytes=KERNEL_BYTES),
        cost_estimate=pl.CostEstimate(
            flops=2 * (shards + 1) * tokens * count * 2 * LANES,
            bytes_accessed=8 * shards * count * LANES,
            transcendentals=0,
        ),
        name="convolve",
    )(own, *held, *toeplitz, skip_gain.reshape(1, channels))


def finish_kernel(scale, value_ref, other_ref, output_ref, grad_ref, filter_out, output_out, grad_out):
    filter_out[...] = (value_ref[...] + other_ref[...]) * scale
    output_out[...] = output_ref[...]
    grad_out[...] = grad_ref[...]


def finish(value, other, output, grad_signal, scale):
    return pl.pallas_call(
        functools.partial(finish_kernel, scale),
        out_shape=[jax.ShapeDtypeStruct(x.shape, x.dtype) for x in (value, output, grad_signal)],
        in_specs=[pl.BlockSpec(memory_space=pltpu.VMEM)] * 4,
        out_specs=[pl.BlockSpec(memory_space=pltpu.VMEM)] * 3,
        compiler_params=pltpu.CompilerParams(vmem_limit_bytes=KERNEL_BYTES),
        name="finish",
    )(value, other, output, grad_signal)


def direct_body(signal, filter_taps, skip_gain, cotangent):
    shards, groups = lax.axis_size("context"), lax.axis_size("chan")
    channels, tokens = signal.shape
    stacked = stack_local(signal, cotangent, filter_taps)
    blocks = gather_blocks(stacked)
    toeplitz = toeplitz_tiles(blocks, shards, channels, tokens)
    value, *held = filter_grad(blocks, shards, channels, tokens)
    other = None
    bits = 1
    while bits < groups:
        if other is not None:
            value = value + other
            value, *toeplitz = lax.optimization_barrier((value, *toeplitz))
        other = lax.ppermute(value, "chan", [(i, i ^ bits) for i in range(groups)])
        bits *= 2
    output, grad_signal = convolve(blocks[0], held, toeplitz, skip_gain, shards, channels, tokens)
    scale = 1.0 / math.sqrt(shards * tokens)
    grad_filter, output, grad_signal = finish(value, other, output, grad_signal, scale)
    return (output, grad_signal, grad_filter.reshape(tokens))


def rotation(first, second, period):
    turned = first * second % period
    return turned.astype(jnp.float32) * (2.0 * math.pi / period)


def table_product(real_part, imag_part, cosine, sine_table):
    return (
        real_part * cosine - imag_part * sine_table,
        real_part * sine_table + imag_part * cosine,
    )


def along_last(real_part, imag_part, angle_table):
    cosine = jnp.cos(angle_table)
    sine_table = jnp.sin(angle_table)
    new_real = jnp.matmul(real_part, cosine, precision=exact_mode) - jnp.matmul(
        imag_part, sine_table, precision=exact_mode
    )
    new_imag = jnp.matmul(real_part, sine_table, precision=exact_mode) + jnp.matmul(
        imag_part, cosine, precision=exact_mode
    )
    return (new_real, new_imag)


def along_slow(real_part, imag_part, angle_table):
    cosine = jnp.cos(angle_table)
    sine_table = jnp.sin(angle_table)
    new_real = jnp.einsum("gsjd,sa->gajd", real_part, cosine, precision=exact_mode) - jnp.einsum(
        "gsjd,sa->gajd", imag_part, sine_table, precision=exact_mode
    )
    new_imag = jnp.einsum(
        "gsjd,sa->gajd", real_part, sine_table, precision=exact_mode
    ) + jnp.einsum("gsjd,sa->gajd", imag_part, cosine, precision=exact_mode)
    return (new_real, new_imag)


def finish_sections(real_part, imag_part, stride, shards, length):
    sources = jnp.arange(shards, dtype=jnp.int32)
    slower = jnp.arange(stride, dtype=jnp.int32)
    slow_angle = -rotation(slower[:, None], slower[None, :], stride)
    real_part, imag_part = along_slow(real_part, imag_part, slow_angle)
    inner_twist = -rotation(slower[:, None, None], sources[None, None, :], length)
    real_part, imag_part = table_product(
        real_part, imag_part, jnp.cos(inner_twist), jnp.sin(inner_twist)
    )
    last_angle = -rotation(sources[:, None], sources[None, :], shards)
    return along_last(real_part, imag_part, last_angle)


def forward(stacked):
    shards = lax.axis_size("context")
    position = lax.axis_index("context")
    signals, length = stacked.shape
    stride = length // shards
    period = 2 * shards * length
    sources = jnp.arange(shards, dtype=jnp.int32)
    slower = jnp.arange(stride, dtype=jnp.int32)
    blocks = stacked.reshape(signals, stride, shards)
    columns = lax.all_to_all(blocks, "context", split_axis=2, concat_axis=2, tiled=True)
    token_ids = shards * slower[:, None] + position
    order = jnp.arange(2 * shards, dtype=jnp.int32)
    first_angle = -rotation(sources[:, None], order[None, :], 2 * shards)
    real_part = jnp.matmul(columns, jnp.cos(first_angle), precision=exact_mode)
    imag_part = jnp.matmul(columns, jnp.sin(first_angle), precision=exact_mode)
    twist = -rotation(token_ids, order[None, :], period)
    real_part, imag_part = table_product(real_part, imag_part, jnp.cos(twist), jnp.sin(twist))
    spectra = jnp.stack([real_part, imag_part]).reshape(2, signals, stride, 2, shards)
    spectra = lax.all_to_all(spectra, "context", split_axis=4, concat_axis=4, tiled=True)
    real_part, imag_part = finish_sections(spectra[0], spectra[1], stride, shards, length)
    return (real_part, imag_part, order)


def inverse(real_part, imag_part, order):
    shards = lax.axis_size("context")
    position = lax.axis_index("context")
    signals, stride = (real_part.shape[0], real_part.shape[1])
    length = stride * shards
    period = 2 * shards * length
    sources = jnp.arange(shards, dtype=jnp.int32)
    slower = jnp.arange(stride, dtype=jnp.int32)
    last_angle = rotation(sources[:, None], sources[None, :], shards)
    real_part, imag_part = along_last(real_part, imag_part, last_angle)
    inner_twist = rotation(slower[:, None, None], sources[None, None, :], length)
    real_part, imag_part = table_product(
        real_part, imag_part, jnp.cos(inner_twist), jnp.sin(inner_twist)
    )
    slow_angle = rotation(slower[:, None], slower[None, :], stride)
    real_part, imag_part = along_slow(real_part, imag_part, slow_angle)
    spectra = lax.all_to_all(
        jnp.stack([real_part, imag_part]), "context", split_axis=4, concat_axis=4, tiled=True
    )
    real_part = spectra[0].reshape(signals, stride, 2 * shards)
    imag_part = spectra[1].reshape(signals, stride, 2 * shards)
    token_ids = shards * slower[:, None] + position
    twist = rotation(token_ids, order[None, :], period)
    real_part, imag_part = table_product(real_part, imag_part, jnp.cos(twist), jnp.sin(twist))
    first_angle = rotation(order[:, None], sources[None, :], 2 * shards)
    cosine = jnp.cos(first_angle)
    sine_table = jnp.sin(first_angle)
    out_real = jnp.matmul(real_part, cosine, precision=exact_mode) - jnp.matmul(
        imag_part, sine_table, precision=exact_mode
    )
    out_imag = jnp.matmul(real_part, sine_table, precision=exact_mode) + jnp.matmul(
        imag_part, cosine, precision=exact_mode
    )
    results = jnp.stack([out_real, out_imag])
    blocks = lax.all_to_all(results, "context", split_axis=3, concat_axis=3, tiled=True)
    return blocks.reshape(blocks.shape[0], signals, length)


def transform_body(signal, filter_taps, skip_gain, cotangent):
    shards = lax.axis_size("context")
    channels, length = signal.shape
    factor = 1.0 / (2 * shards * length * math.sqrt(shards * length))
    stacked = jnp.concatenate([signal, cotangent, filter_taps[None, :]], axis=0)
    real_part, imag_part, order = forward(stacked)
    sig_re = real_part[:channels]
    sig_im = imag_part[:channels]
    cot_re = real_part[channels : 2 * channels]
    cot_im = imag_part[channels : 2 * channels]
    fil_re = real_part[2 * channels :]
    fil_im = imag_part[2 * channels :]
    out_re = sig_re * fil_re - sig_im * fil_im
    out_im = sig_re * fil_im + sig_im * fil_re
    back_re = cot_re * fil_re + cot_im * fil_im
    back_im = cot_im * fil_re - cot_re * fil_im
    grad_re = jnp.sum(cot_re * sig_re + cot_im * sig_im, axis=0, keepdims=True)
    grad_im = jnp.sum(cot_im * sig_re - cot_re * sig_im, axis=0, keepdims=True)
    restored = inverse(
        jnp.concatenate([out_re - back_im, grad_re], axis=0),
        jnp.concatenate([out_im + back_re, grad_im], axis=0),
        order,
    )
    conv_out = restored[0, :channels]
    conv_back = restored[1, :channels]
    partial_value = restored[0, channels]
    output = conv_out * factor + skip_gain[:, None] * signal
    grad_signal = conv_back * factor + skip_gain[:, None] * cotangent
    grad_filter = lax.psum(partial_value * factor, "chan")
    return (output, grad_signal, grad_filter)


def fits_direct(channels, tokens, shards):
    held = 4 * shards * tokens * (2 * channels + 1)
    scratch = 16 * shards * tokens * channels + 4 * (shards * tokens + LANES) * LANES
    groups = lax.axis_size("chan")
    whole = groups & (groups - 1) == 0 and channels % PACKED_ROWS == 0 and tokens % (8 * LANES) == 0 and shards & (shards - 1) == 0
    return whole and shards == SHARDS and 2 * held + scratch < KERNEL_BYTES


def body(signal, filter_taps, skip_gain, cotangent):
    channels, tokens = signal.shape
    if fits_direct(channels, tokens, lax.axis_size("context")):
        return direct_body(signal, filter_taps, skip_gain, cotangent)
    return transform_body(signal, filter_taps, skip_gain, cotangent)


def solution(mesh):
    return jax.shard_map(
        body,
        mesh=mesh,
        in_specs=(P("chan", "context"), P("context"), P("chan"), P("chan", "context")),
        out_specs=(P("chan", "context"), P("chan", "context"), P("context")),
        check_vma=False,
    )
```

```python
import functools
import math

import jax
import jax.numpy as jnp
from jax import lax
from jax.experimental import pallas as pl
from jax.experimental.pallas import tpu as pltpu
from jax.sharding import PartitionSpec as P

exact_mode = lax.Precision.HIGHEST

SHARDS = 8
FLIPS = ((0, 0), (2, 4), (6, 6), (4, 2))
LANES = 128
BLOCK = 256
PACKED_ROWS = 16
KERNEL_BYTES = 16 * 1024 * 1024


def halves(value):
    high = value.astype(jnp.bfloat16)
    low = (value - high.astype(jnp.float32)).astype(jnp.bfloat16)
    return high, low


def dot(left, right, left_dim, right_dim):
    return lax.dot_general(
        left, right, (((left_dim,), (right_dim,)), ((), ())), preferred_element_type=jnp.float32
    )


def stack_kernel(signal_ref, cotangent_ref, taps_ref, out_ref):
    channels, tokens = signal_ref.shape
    row = 0
    for source in (signal_ref, cotangent_ref):
        for tile in range(tokens // LANES):
            out_ref[row : row + channels, :] = source[:, tile * LANES : (tile + 1) * LANES]
            row += channels
    out_ref[row:, :] = taps_ref[...]


def stack_local(signal, cotangent, taps):
    channels, tokens = signal.shape
    rows = (2 * channels * tokens + tokens) // LANES
    return pl.pallas_call(
        stack_kernel,
        out_shape=pltpu.VMEM((rows, LANES), jnp.float32),
        in_specs=[pl.BlockSpec(memory_space=pltpu.VMEM)] * 3,
        out_specs=pl.BlockSpec(memory_space=pltpu.VMEM),
        name="stack_local",
    )(signal, cotangent, taps.reshape(tokens // LANES, LANES))


def source_index(me, entry):
    core = me % 2 if entry % 2 == 0 else 1 - me % 2
    even, odd = FLIPS[entry // 2]
    return me ^ (even + (odd - even) * core + entry % 2)


def gather_blocks(stacked):
    def fetched(value, entry):
        return lax.ppermute(value, "context", [(source_index(i, entry), i) for i in range(SHARDS)])

    found = {0: stacked}
    for entry in range(2, SHARDS, 2):
        found[entry] = fetched(stacked, entry)
    for entry in range(0, SHARDS, 2):
        found[entry + 1] = fetched(found[entry], 1)
    return [found[entry] for entry in range(SHARDS)]


def place_rows(block_ref, first, index, channels, tokens, ref, start):
    tiles = tokens // LANES
    for tile in range(tiles):
        rows = first + tile * channels
        both = jnp.concatenate(halves(block_ref[rows : rows + channels, :]), axis=0)
        at = pl.multiple_of((index * tiles + tile) * 2 * channels + start, PACKED_ROWS)
        ref[pl.ds(at, 2 * channels), :] = both


def paired_tiles(ref, start, count, channels, half):
    def rows(tile):
        at = pl.multiple_of((start + tile) * 2 * channels + half * channels, PACKED_ROWS)
        return ref[pl.ds(at, channels), :]

    return jnp.concatenate(
        [jnp.concatenate([rows(tile), rows(tile + 1)], axis=1) for tile in range(0, count, 2)], axis=0
    )


def filter_grad_kernel(shards, channels, tokens, *refs):
    blocks, out_ref, sig, cot, folded = refs[:shards], *refs[shards:]
    me = lax.axis_index("context")
    per, tiles = tokens // BLOCK, tokens // LANES
    count = 2 * tiles * channels
    rows = shards * count
    sig[:count, :] = jnp.zeros((count, LANES), jnp.bfloat16)
    cot[rows:, :] = jnp.zeros((rows, LANES), jnp.bfloat16)
    for bits in range(shards):
        index = source_index(me, bits)
        place_rows(blocks[bits], 0, index, channels, tokens, sig, count)
        place_rows(blocks[bits], channels * tiles, index, channels, tokens, cot, 0)
    held = [paired_tiles(sig, tiles, shards * tiles, channels, half) for half in range(2)]
    for lag in range(per + 1):
        window = [
            paired_tiles(cot, me * tiles + 2 * lag, shards * tiles, channels, half) for half in range(2)
        ]
        folded[:, lag * BLOCK : (lag + 1) * BLOCK] = dot(jnp.concatenate([held[0], held[0], held[1]], axis=0), jnp.concatenate([window[0], window[1], window[0]], axis=0), 0, 0)
    width = (per + 1) * BLOCK - LANES
    total = None
    for group in range(LANES // 8):
        part = (
            folded[8 * group : 8 * group + 8, :width]
            + folded[LANES + 8 * group : LANES + 8 * group + 8, LANES:]
        )
        if group:
            part = pltpu.roll(part, width - 8 * group, 1)
        total = part if total is None else total + part
    row = lax.broadcasted_iota(jnp.int32, total.shape, 0)
    for step in (1, 2, 4):
        total = jnp.where((row & step) != 0, pltpu.roll(total, width - step, 1), total)
    out_ref[...] = jnp.sum(total, axis=0, keepdims=True)[:, :tokens]


def filter_grad(blocks, shards, channels, tokens):
    per = tokens // BLOCK
    rows = shards * per * channels
    return pl.pallas_call(
        functools.partial(filter_grad_kernel, shards, channels, tokens),
        out_shape=[
            jax.ShapeDtypeStruct((1, tokens), jnp.float32),
            pltpu.VMEM((4 * rows // shards * (shards + 1), LANES), jnp.bfloat16),
            pltpu.VMEM((8 * rows, LANES), jnp.bfloat16),
        ],
        in_specs=[pl.BlockSpec(memory_space=pltpu.VMEM)] * shards,
        out_specs=[pl.BlockSpec(memory_space=pltpu.VMEM)] * 3,
        scratch_shapes=[pltpu.VMEM((BLOCK, (per + 1) * BLOCK), jnp.float32)],
        compiler_params=pltpu.CompilerParams(vmem_limit_bytes=KERNEL_BYTES),
        cost_estimate=pl.CostEstimate(
            flops=2 * 3 * (per + 1) * rows * BLOCK * BLOCK, bytes_accessed=4 * rows * BLOCK * 2, transcendentals=0
        ),
        name="filter_grad",
    )(*blocks)


def convolve_block(held, me, tiles, channels, toe_high, toe_low, block, adjoint):
    count = 2 * tiles * channels
    lags = [block * tiles + n for n in range(tiles)]

    def window(lag):
        tile = me * tiles + lag if adjoint else (me + 1) * tiles - lag
        return held[pl.ds(pl.multiple_of(tile * 2 * channels, PACKED_ROWS), count), :]

    side = 0 if adjoint else 1
    left = jnp.concatenate([window(lag) for lag in lags], axis=1)
    pairs = [jnp.concatenate([toe_high[lag + 1], toe_low[lag + 1]], axis=side) for lag in lags]
    return dot(left, jnp.concatenate(pairs, axis=1 - side), 1, 1 - side)


def toeplitz_kernel(shards, channels, tokens, *refs):
    blocks, high_ref, low_ref, taps, skew = refs[:shards], *refs[shards:]
    me = lax.axis_index("context")
    tiles = tokens // LANES
    first = 2 * channels * tiles
    taps[0] = jnp.zeros((tiles, LANES), jnp.float32)
    for bits in range(shards):
        taps[source_index(me, bits) + 1] = blocks[bits][first : first + tiles, :]
    high_ref[0] = jnp.zeros((LANES, LANES), jnp.bfloat16)
    low_ref[0] = jnp.zeros((LANES, LANES), jnp.bfloat16)
    width = (tiles + 1) * LANES

    for step in range(shards):
        last, sheet = taps[step], taps[step + 1]
        lines = [last[tiles - 1 : tiles, :]] + [sheet[n : n + 1, :] for n in range(tiles)]
        lean = jnp.concatenate([jnp.broadcast_to(line, (8, LANES)) for line in lines], axis=1)
        lean = pltpu.roll(lean, 0, 1, stride=1, stride_axis=0)
        skew[step] = lean

    def build(step, carry):
        skewed = skew[step]
        for group in range(LANES // PACKED_ROWS):
            top, bottom = (
                pltpu.roll(skewed, PACKED_ROWS * group + rows, 1) if group + rows else skewed
                for rows in (0, 8)
            )
            pair = halves(jnp.concatenate([top, bottom], axis=0))
            for ref, part in zip((high_ref, low_ref), pair):
                for tile in range(tiles):
                    ref[
                        step * tiles + tile + 1, group * PACKED_ROWS : (group + 1) * PACKED_ROWS, :
                    ] = part[:, (tile + 1) * LANES : (tile + 2) * LANES]
        return carry

    lax.fori_loop(0, shards, build, 0, unroll=min(4, shards))


def toeplitz_tiles(blocks, shards, channels, tokens):
    tiles = tokens // LANES
    shape = (shards * tiles + 1, LANES, LANES)
    return pl.pallas_call(
        functools.partial(toeplitz_kernel, shards, channels, tokens),
        out_shape=[pltpu.VMEM(shape, jnp.bfloat16)] * 2,
        in_specs=[pl.BlockSpec(memory_space=pltpu.VMEM)] * shards,
        out_specs=[pl.BlockSpec(memory_space=pltpu.VMEM)] * 2,
        scratch_shapes=[pltpu.VMEM((shards + 1, tiles, LANES), jnp.float32), pltpu.VMEM((shards, 8, (tiles + 1) * LANES), jnp.float32)],
        compiler_params=pltpu.CompilerParams(vmem_limit_bytes=KERNEL_BYTES),
        cost_estimate=pl.CostEstimate(
            flops=16 * shape[0] * LANES * LANES, bytes_accessed=4 * shape[0] * LANES * LANES, transcendentals=0
        ),
        name="toeplitz_tiles",
    )(*blocks)


def convolve_kernel(shards, channels, tokens, *refs):
    own_ref, sig, cot, toe_high, toe_low, gain_ref, out_ref, back_ref, conv, back = refs
    me = lax.axis_index("context")
    tiles = tokens // LANES

    def total(held, blocks, adjoint):
        parts = [
            convolve_block(held, me, tiles, channels, toe_high, toe_low, block, adjoint) for block in range(blocks)
        ]
        return sum(parts[1:], parts[0])

    def run(index):
        conv[...] = total(sig, index + 1, False)
        back[...] = total(cot, shards - index, True)

    for index in range(shards):
        pl.when(me == index)(functools.partial(run, index))
    factor = 1.0 / math.sqrt(shards * tokens)
    square_row = lax.broadcasted_iota(jnp.int32, (channels, channels), 0)
    square_lane = lax.broadcasted_iota(jnp.int32, (channels, channels), 1)
    gain = jnp.sum(
        jnp.where(square_row == square_lane, jnp.broadcast_to(gain_ref[...], (channels, channels)), 0.0),
        axis=1,
        keepdims=True,
    )
    for tile in range(tiles):
        lanes = slice(tile * LANES, (tile + 1) * LANES)
        for ref, value, first in ((out_ref, conv, 0), (back_ref, back, tiles)):
            own = own_ref[(first + tile) * channels : (first + tile + 1) * channels, :]
            top = tile * 2 * channels
            both = value[top : top + channels, :] + value[top + channels : top + 2 * channels, :]
            ref[:, lanes] = (both[:, :LANES] + both[:, LANES:]) * factor + gain * own


def convolve(own, held, toeplitz, skip_gain, shards, channels, tokens):
    count = 2 * channels * tokens // LANES
    return pl.pallas_call(
        functools.partial(convolve_kernel, shards, channels, tokens),
        out_shape=[pltpu.VMEM((channels, tokens), jnp.float32)] * 2,
        in_specs=[pl.BlockSpec(memory_space=pltpu.VMEM)] * 6,
        out_specs=[pl.BlockSpec(memory_space=pltpu.VMEM)] * 2,
        scratch_shapes=[pltpu.VMEM((count, 2 * LANES), jnp.float32)] * 2,
        compiler_params=pltpu.CompilerParams(vmem_limit_bytes=KERNEL_BYTES),
        cost_estimate=pl.CostEstimate(
            flops=2 * (shards + 1) * tokens * count * 2 * LANES,
            bytes_accessed=8 * shards * count * LANES,
            transcendentals=0,
        ),
        name="convolve",
    )(own, *held, *toeplitz, skip_gain.reshape(1, channels))


def finish_kernel(scale, value_ref, other_ref, output_ref, grad_ref, filter_out, output_out, grad_out):
    filter_out[...] = (value_ref[...] + other_ref[...]) * scale
    output_out[...] = output_ref[...]
    grad_out[...] = grad_ref[...]


def finish(value, other, output, grad_signal, scale):
    return pl.pallas_call(
        functools.partial(finish_kernel, scale),
        out_shape=[jax.ShapeDtypeStruct(x.shape, x.dtype) for x in (value, output, grad_signal)],
        in_specs=[pl.BlockSpec(memory_space=pltpu.VMEM)] * 4,
        out_specs=[pl.BlockSpec(memory_space=pltpu.VMEM)] * 3,
        compiler_params=pltpu.CompilerParams(vmem_limit_bytes=KERNEL_BYTES),
        name="finish",
    )(value, other, output, grad_signal)


def direct_body(signal, filter_taps, skip_gain, cotangent):
    shards, groups = lax.axis_size("context"), lax.axis_size("chan")
    channels, tokens = signal.shape
    stacked = stack_local(signal, cotangent, filter_taps)
    blocks = gather_blocks(stacked)
    value, *held = filter_grad(blocks, shards, channels, tokens)
    toeplitz = toeplitz_tiles(blocks, shards, channels, tokens)
    other = None
    bits = groups // 2
    while bits:
        if other is not None:
            value = value + other
            value, *toeplitz = lax.optimization_barrier((value, *toeplitz))
        other = lax.ppermute(value, "chan", [(i, i ^ bits) for i in range(groups)])
        bits //= 2
    output, grad_signal = convolve(blocks[0], held, toeplitz, skip_gain, shards, channels, tokens)
    scale = 1.0 / math.sqrt(shards * tokens)
    grad_filter, output, grad_signal = finish(value, other, output, grad_signal, scale)
    return (output, grad_signal, grad_filter.reshape(tokens))


def rotation(first, second, period):
    turned = first * second % period
    return turned.astype(jnp.float32) * (2.0 * math.pi / period)


def table_product(real_part, imag_part, cosine, sine_table):
    return (
        real_part * cosine - imag_part * sine_table,
        real_part * sine_table + imag_part * cosine,
    )


def along_last(real_part, imag_part, angle_table):
    cosine = jnp.cos(angle_table)
    sine_table = jnp.sin(angle_table)
    new_real = jnp.matmul(real_part, cosine, precision=exact_mode) - jnp.matmul(
        imag_part, sine_table, precision=exact_mode
    )
    new_imag = jnp.matmul(real_part, sine_table, precision=exact_mode) + jnp.matmul(
        imag_part, cosine, precision=exact_mode
    )
    return (new_real, new_imag)


def along_slow(real_part, imag_part, angle_table):
    cosine = jnp.cos(angle_table)
    sine_table = jnp.sin(angle_table)
    new_real = jnp.einsum("gsjd,sa->gajd", real_part, cosine, precision=exact_mode) - jnp.einsum(
        "gsjd,sa->gajd", imag_part, sine_table, precision=exact_mode
    )
    new_imag = jnp.einsum(
        "gsjd,sa->gajd", real_part, sine_table, precision=exact_mode
    ) + jnp.einsum("gsjd,sa->gajd", imag_part, cosine, precision=exact_mode)
    return (new_real, new_imag)


def finish_sections(real_part, imag_part, stride, shards, length):
    sources = jnp.arange(shards, dtype=jnp.int32)
    slower = jnp.arange(stride, dtype=jnp.int32)
    slow_angle = -rotation(slower[:, None], slower[None, :], stride)
    real_part, imag_part = along_slow(real_part, imag_part, slow_angle)
    inner_twist = -rotation(slower[:, None, None], sources[None, None, :], length)
    real_part, imag_part = table_product(
        real_part, imag_part, jnp.cos(inner_twist), jnp.sin(inner_twist)
    )
    last_angle = -rotation(sources[:, None], sources[None, :], shards)
    return along_last(real_part, imag_part, last_angle)


def forward(stacked):
    shards = lax.axis_size("context")
    position = lax.axis_index("context")
    signals, length = stacked.shape
    stride = length // shards
    period = 2 * shards * length
    sources = jnp.arange(shards, dtype=jnp.int32)
    slower = jnp.arange(stride, dtype=jnp.int32)
    blocks = stacked.reshape(signals, stride, shards)
    columns = lax.all_to_all(blocks, "context", split_axis=2, concat_axis=2, tiled=True)
    token_ids = shards * slower[:, None] + position
    order = jnp.arange(2 * shards, dtype=jnp.int32)
    first_angle = -rotation(sources[:, None], order[None, :], 2 * shards)
    real_part = jnp.matmul(columns, jnp.cos(first_angle), precision=exact_mode)
    imag_part = jnp.matmul(columns, jnp.sin(first_angle), precision=exact_mode)
    twist = -rotation(token_ids, order[None, :], period)
    real_part, imag_part = table_product(real_part, imag_part, jnp.cos(twist), jnp.sin(twist))
    spectra = jnp.stack([real_part, imag_part]).reshape(2, signals, stride, 2, shards)
    spectra = lax.all_to_all(spectra, "context", split_axis=4, concat_axis=4, tiled=True)
    real_part, imag_part = finish_sections(spectra[0], spectra[1], stride, shards, length)
    return (real_part, imag_part, order)


def inverse(real_part, imag_part, order):
    shards = lax.axis_size("context")
    position = lax.axis_index("context")
    signals, stride = (real_part.shape[0], real_part.shape[1])
    length = stride * shards
    period = 2 * shards * length
    sources = jnp.arange(shards, dtype=jnp.int32)
    slower = jnp.arange(stride, dtype=jnp.int32)
    last_angle = rotation(sources[:, None], sources[None, :], shards)
    real_part, imag_part = along_last(real_part, imag_part, last_angle)
    inner_twist = rotation(slower[:, None, None], sources[None, None, :], length)
    real_part, imag_part = table_product(
        real_part, imag_part, jnp.cos(inner_twist), jnp.sin(inner_twist)
    )
    slow_angle = rotation(slower[:, None], slower[None, :], stride)
    real_part, imag_part = along_slow(real_part, imag_part, slow_angle)
    spectra = lax.all_to_all(
        jnp.stack([real_part, imag_part]), "context", split_axis=4, concat_axis=4, tiled=True
    )
    real_part = spectra[0].reshape(signals, stride, 2 * shards)
    imag_part = spectra[1].reshape(signals, stride, 2 * shards)
    token_ids = shards * slower[:, None] + position
    twist = rotation(token_ids, order[None, :], period)
    real_part, imag_part = table_product(real_part, imag_part, jnp.cos(twist), jnp.sin(twist))
    first_angle = rotation(order[:, None], sources[None, :], 2 * shards)
    cosine = jnp.cos(first_angle)
    sine_table = jnp.sin(first_angle)
    out_real = jnp.matmul(real_part, cosine, precision=exact_mode) - jnp.matmul(
        imag_part, sine_table, precision=exact_mode
    )
    out_imag = jnp.matmul(real_part, sine_table, precision=exact_mode) + jnp.matmul(
        imag_part, cosine, precision=exact_mode
    )
    results = jnp.stack([out_real, out_imag])
    blocks = lax.all_to_all(results, "context", split_axis=3, concat_axis=3, tiled=True)
    return blocks.reshape(blocks.shape[0], signals, length)


def transform_body(signal, filter_taps, skip_gain, cotangent):
    shards = lax.axis_size("context")
    channels, length = signal.shape
    factor = 1.0 / (2 * shards * length * math.sqrt(shards * length))
    stacked = jnp.concatenate([signal, cotangent, filter_taps[None, :]], axis=0)
    real_part, imag_part, order = forward(stacked)
    sig_re = real_part[:channels]
    sig_im = imag_part[:channels]
    cot_re = real_part[channels : 2 * channels]
    cot_im = imag_part[channels : 2 * channels]
    fil_re = real_part[2 * channels :]
    fil_im = imag_part[2 * channels :]
    out_re = sig_re * fil_re - sig_im * fil_im
    out_im = sig_re * fil_im + sig_im * fil_re
    back_re = cot_re * fil_re + cot_im * fil_im
    back_im = cot_im * fil_re - cot_re * fil_im
    grad_re = jnp.sum(cot_re * sig_re + cot_im * sig_im, axis=0, keepdims=True)
    grad_im = jnp.sum(cot_im * sig_re - cot_re * sig_im, axis=0, keepdims=True)
    restored = inverse(
        jnp.concatenate([out_re - back_im, grad_re], axis=0),
        jnp.concatenate([out_im + back_re, grad_im], axis=0),
        order,
    )
    conv_out = restored[0, :channels]
    conv_back = restored[1, :channels]
    partial_value = restored[0, channels]
    output = conv_out * factor + skip_gain[:, None] * signal
    grad_signal = conv_back * factor + skip_gain[:, None] * cotangent
    grad_filter = lax.psum(partial_value * factor, "chan")
    return (output, grad_signal, grad_filter)


def fits_direct(channels, tokens, shards):
    held = 4 * shards * tokens * (2 * channels + 1)
    scratch = 16 * shards * tokens * channels + 4 * (shards * tokens + LANES) * LANES
    groups = lax.axis_size("chan")
    whole = groups & (groups - 1) == 0 and channels % PACKED_ROWS == 0 and tokens % (8 * LANES) == 0 and shards & (shards - 1) == 0
    return whole and shards == SHARDS and 2 * held + scratch < KERNEL_BYTES


def body(signal, filter_taps, skip_gain, cotangent):
    channels, tokens = signal.shape
    if fits_direct(channels, tokens, lax.axis_size("context")):
        return direct_body(signal, filter_taps, skip_gain, cotangent)
    return transform_body(signal, filter_taps, skip_gain, cotangent)


def solution(mesh):
    return jax.shard_map(
        body,
        mesh=mesh,
        in_specs=(P("chan", "context"), P("context"), P("chan"), P("chan", "context")),
        out_specs=(P("chan", "context"), P("chan", "context"), P("context")),
        check_vma=False,
    )
```
